32 devices in a mesh: dp: 4 (over x, core), seq: 8 (over z, y).
Axes of the slice: x: 2, y: 2, z: 4, core: 2. Of those that a mesh axis runs over, the one named last changes fastest.
Arguments:
- tokens: bfloat16 [4, 6144, 2560], P('dp', 'seq'), may hold values from -6 to 6
- w_xbc: bfloat16 [2560, 2816], P(('dp', 'seq')), may hold values from -0.125 to 0.125
- conv_weight: float32 [4, 2816], replicated, may hold values from -3 to 3
- conv_bias: float32 [2816], replicated, may hold values from -2 to 2
- a_log: float32 [40], replicated, may hold values from -13 to -3
- dt_in: float32 [4, 40, 6144], P('dp', None, 'seq'), may hold values from -2 to 49152
- d_skip: float32 [40], replicated, may hold values from 0.5 to 1.5
- norm_gain: float32 [2560], replicated, may hold values from 0.25 to 1.75
Outputs:
- normed: bfloat16 [4, 6144, 2560], P('dp', 'seq')
The draws below stay inside these ranges and needn't reach their ends.
All inputs are finite; a program needn't handle non-finite values.
Results may differ from the reference program's by a relative error of at most 0.012.
Values may be sent and summed in bfloat16 or wider, within the bound.
No kernel may reach another device: no remote copies, remote signals or barrier semaphores. Data moves between devices by JAX's collectives and lax.ppermute only.
A program may use at most 128 MiB of HBM per device.

```python
import math
import jax
import jax.numpy as jnp
from jax import lax

D = 2560
H = 40
P_SIZE = 64
N = 128
CONV = 4
GROUP = 256
TOK_DEV = 768
DXBC = 2816
SEQLEN = 6144
DESIGNS = 4


def head_rates(key):
    key_class, key_fast, key_slow = jax.random.split(jax.random.fold_in(key, 11), 3)
    fast_share = 5
    is_fast = jax.random.randint(key_class, (H,), 0, 10) < fast_share
    fast_rate = jnp.exp(jax.random.uniform(key_fast, (H,), jnp.float32, math.log(1.0 / 50.0), math.log(1.0 / 30.0)))
    slow_rate = jnp.exp(jax.random.uniform(key_slow, (H,), jnp.float32, math.log(0.1), math.log(0.4))) / SEQLEN
    return jnp.where(is_fast, fast_rate, slow_rate)


def draw_a_log(key, part):
    return jnp.log(head_rates(key)).astype(jnp.float32)


def draw_dt_in(key, part):
    rates = head_rates(key)
    key_block, key_jitter, key_place, key_loss = jax.random.split(jax.random.fold_in(key, 23), 4)
    shard_count = SEQLEN // TOK_DEV
    block_factor = jnp.exp(jax.random.uniform(key_block, (DESIGNS, 1, shard_count, 1), jnp.float32, math.log(0.5), math.log(2.0)))
    jitter = jnp.exp(jax.random.uniform(key_jitter, (DESIGNS, H, shard_count, TOK_DEV), jnp.float32, math.log(0.5), math.log(2.0)))
    target = (block_factor * jitter).reshape(DESIGNS, H, SEQLEN)
    places = jax.random.randint(key_place, (DESIGNS, 2), 0, SEQLEN)
    hit = jnp.any(jnp.arange(SEQLEN)[None, None, :] == places[:, :, None], axis=1)
    loss = jax.random.uniform(key_loss, (DESIGNS, 1, SEQLEN), jnp.float32, 0.223, 0.693)
    target = jnp.where(hit[:, None, :], loss / rates[None, :, None], target)
    inverse = jnp.where(target > 20.0, target, jnp.log(jnp.expm1(jnp.minimum(target, 20.0))))
    return inverse.astype(jnp.float32)


def levels(stream_key, dims, shards, smallest, top_value):
    gain = 1.0
    for position, blocks in shards:
        draws = jax.random.uniform(jax.random.fold_in(jax.random.fold_in(stream_key, 6), position), (blocks,), jnp.float32, smallest / len(shards), top_value / len(shards))
        gain = gain * jnp.repeat(jnp.exp(draws), dims[position] // blocks).reshape((-1,) + (1,) * (len(dims) - 1 - position))
    return gain


def bell_draw(key, dims, width, limit, cuts=(), kind=jnp.bfloat16):
    array = width * jax.random.normal(key, dims, jnp.float32)
    if cuts:
        array = array * levels(key, dims, cuts, -0.22, 0.18)
    return jnp.clip(array, -limit, limit).astype(kind)


def setup_inputs(seed: int = 0) -> dict:
    key_of = jax.random.split(jax.random.key(seed), 9)
    return {
        "tokens": bell_draw(key_of[0], (DESIGNS, SEQLEN, D), 1.0, 6.0, ((0, 4), (1, 8))),
        "w_xbc": bell_draw(key_of[1], (D, DXBC), D ** -0.5, 0.125, ((0, 32),)),
        "conv_weight": bell_draw(key_of[2], (CONV, DXBC), 4 ** -0.5, 3.0, (), jnp.float32),
        "conv_bias": bell_draw(key_of[3], (DXBC,), 0.3, 2.0, (), jnp.float32),
        "a_log": draw_a_log(jax.random.fold_in(key_of[8], 71), 0),
        "dt_in": draw_dt_in(jax.random.fold_in(key_of[8], 71), 0),
        "d_skip": jnp.clip(jax.random.uniform(key_of[6], (H,), jnp.float32, 0.5, 1.5), 0.5, 1.5),
        "norm_gain": jnp.clip(1.0 + 0.15 * jax.random.normal(key_of[7], (H * P_SIZE,), jnp.float32), 0.25, 1.75),
    }


def span_terms(x_block, b_block, c_block, dt_block, decay_block):
    heads = dt_block.shape[0]
    length = dt_block.shape[1]
    x_heads = x_block.astype(jnp.float32).reshape(length, heads, -1)
    b_float = b_block.astype(jnp.float32)
    cumul = jnp.cumsum(decay_block, axis=1)
    spread = cumul[:, :, None] - cumul[:, None, :]
    lower = jnp.arange(length)[:, None] >= jnp.arange(length)[None, :]
    decay_mat = jnp.exp(jnp.where(lower[None], spread, -jnp.inf))
    scores = jnp.dot(c_block, b_block.T, preferred_element_type=jnp.float32)
    mixing = decay_mat * scores[None] * dt_block[:, None, :]
    y_inner = jnp.einsum('hij,jhp->ihp', mixing, x_heads, precision=lax.Precision.HIGH)
    tail_weight = jnp.exp(cumul[:, -1:] - cumul) * dt_block
    weighted = tail_weight.T[:, :, None] * x_heads
    span_state = jnp.einsum('jhp,jn->hpn', weighted, b_float, precision=lax.Precision.HIGH)
    return (y_inner, span_state, cumul[:, -1], cumul)

def design_pass(design_tokens, design_dt, w_xbc, conv_weight, conv_bias, a_log, d_skip, norm_gain):
    xbc = jnp.dot(design_tokens, w_xbc, preferred_element_type=jnp.float32).astype(jnp.bfloat16)
    padded = jnp.concatenate([jnp.zeros((CONV - 1, DXBC), jnp.bfloat16), xbc], axis=0)
    accum = conv_bias[None, :] + jnp.zeros((SEQLEN, DXBC), jnp.float32)
    for tap_index in range(CONV):
        accum = accum + conv_weight[tap_index][None, :] * padded[tap_index:tap_index + SEQLEN].astype(jnp.float32)
    conv_out = jax.nn.silu(accum).astype(jnp.bfloat16)
    width_x = H * P_SIZE
    x_all = conv_out[:, :width_x]
    b_all = conv_out[:, width_x:width_x + N]
    c_all = conv_out[:, width_x + N:]
    step_size = jax.nn.softplus(design_dt)
    log_decay = -jnp.exp(a_log)[:, None] * step_size
    blocks = SEQLEN // GROUP
    x_blocks = x_all.reshape(blocks, GROUP, width_x)
    b_blocks = b_all.reshape(blocks, GROUP, N)
    c_blocks = c_all.reshape(blocks, GROUP, N)
    dt_blocks = step_size.reshape(H, blocks, GROUP).transpose(1, 0, 2)
    decay_blocks = log_decay.reshape(H, blocks, GROUP).transpose(1, 0, 2)

    def advance(state, inputs):
        x_block, b_block, c_block, dt_block, decay_block = inputs
        y_inner, span_state, totals, cumul = span_terms(x_block, b_block, c_block, dt_block, decay_block)
        from_state = jnp.einsum('in,hpn->ihp', c_block.astype(jnp.float32), state, precision=lax.Precision.HIGH)
        y_block = y_inner + jnp.exp(cumul).T[:, :, None] * from_state
        new_state = jnp.exp(totals)[:, None, None] * state + span_state
        return (new_state, y_block)
    start_state = jnp.zeros((H, P_SIZE, N), jnp.float32)
    final_state, y_blocks = lax.scan(advance, start_state, (x_blocks, b_blocks, c_blocks, dt_blocks, decay_blocks))
    x_heads = x_all.astype(jnp.float32).reshape(SEQLEN, H, P_SIZE)
    ssd = y_blocks.reshape(SEQLEN, H, P_SIZE) + d_skip[None, :, None] * x_heads
    mean_sq = lax.optimization_barrier(jnp.mean(ssd * ssd, axis=-1, keepdims=True))
    scaled = ssd * lax.rsqrt(mean_sq + 1e-05) * norm_gain.reshape(H, P_SIZE)[None]
    return scaled.reshape(SEQLEN, H * P_SIZE).astype(jnp.bfloat16)

def reference(tokens, w_xbc, conv_weight, conv_bias, a_log, dt_in, d_skip, norm_gain):

    def one_design(pair):
        return design_pass(pair[0], pair[1], w_xbc, conv_weight, conv_bias, a_log, d_skip, norm_gain)
    return lax.map(one_design, (tokens, dt_in))
```

```python
import jax
import jax.numpy as jnp
from jax import lax
from jax.experimental import pallas as pl
from jax.experimental.pallas import tpu as pltpu
from jax.sharding import PartitionSpec as P

SPAN = 128
TILE = 256
RIM = 16
VMEM = 56 * 1024 * 1024


def halves(left, right):
    lane = lax.broadcasted_iota(jnp.int32, left.shape, 1)
    return jnp.where(lane < left.shape[1] // 2, left, right)


def spread(columns, index):
    return jnp.broadcast_to(columns[:, index : index + 1], (columns.shape[0], SPAN))


def convolve(rows_ref, taps_ref, base, left):
    cols = pl.ds(left, SPAN)
    accum = jnp.broadcast_to(taps_ref[4:5, cols], (SPAN, SPAN))
    for tap in range(4):
        accum = accum + taps_ref[tap : tap + 1, cols] * rows_ref[pl.ds(base + RIM - 3 + tap, SPAN), cols]
    return 0.5 * accum * (1.0 + jnp.tanh(0.5 * accum))


def project(tok_ref, w_ref, rows_ref):
    out = jnp.dot(tok_ref[...], w_ref[...], preferred_element_type=jnp.float32)
    rows_ref[...] = out.astype(jnp.bfloat16).astype(jnp.float32)


def bc_kernel(tok_ref, w_ref, taps_ref, c_ref, bt_ref, scores_ref, rows_ref):
    project(tok_ref, w_ref, rows_ref)
    row = lax.broadcasted_iota(jnp.int32, (SPAN, SPAN), 0)
    col = lax.broadcasted_iota(jnp.int32, (SPAN, SPAN), 1)
    for block in range(scores_ref.shape[0]):
        at = block * SPAN
        b_t = convolve(rows_ref, taps_ref, at, 0).T.astype(jnp.bfloat16)
        c_rows = convolve(rows_ref, taps_ref, at, SPAN).astype(jnp.bfloat16)
        bt_ref[:, pl.ds(at, SPAN)] = b_t
        c_ref[pl.ds(at, SPAN), :] = c_rows
        scores = jnp.dot(c_rows, b_t, preferred_element_type=jnp.float32)
        scores_ref[block] = jnp.where(row >= col, scores, 0.0)


def ssd_kernel(tok_ref, w_ref, taps_ref, c_ref, bt_ref, scores_ref, cols_ref, rowsv_ref, lanes_ref, y_ref, state_ref, rows_ref):
    project(tok_ref, w_ref, rows_ref)
    blocks = scores_ref.shape[0]
    for pair in range(TILE // SPAN):
        left = pair * SPAN
        state = None
        for block in range(blocks):
            at = block * SPAN
            here = pl.ds(at, SPAN)
            cols = cols_ref[0, here, :]
            first, second = spread(cols, 2 * pair), spread(cols, 2 * pair + 1)
            dts = halves(spread(cols, 4 + 2 * pair), spread(cols, 5 + 2 * pair))
            x = convolve(rows_ref, taps_ref, at, left).astype(jnp.bfloat16).astype(jnp.float32)
            xdt = x * dts
            scores = scores_ref[block]
            mix = []
            for head, cum in enumerate((first, second)):
                across = rowsv_ref[0, 2 * pair + head : 2 * pair + head + 1, here]
                mix.append((jnp.exp(jnp.minimum(cum - across, 0.0)) * scores).astype(jnp.bfloat16))
            zero = jnp.zeros_like(xdt)
            stacked = jnp.concatenate([halves(xdt, zero), halves(zero, xdt)], axis=0).astype(jnp.bfloat16)
            y = jnp.dot(jnp.concatenate(mix, axis=1), stacked, preferred_element_type=jnp.float32)
            cum = halves(first, second)
            total = lanes_ref[0, block : block + 1, pl.ds(left, SPAN)]
            if state is not None:
                carried = jnp.dot(c_ref[here, :], state.astype(jnp.bfloat16), preferred_element_type=jnp.float32)
                y = y + jnp.exp(cum) * carried
            y_ref[here, pl.ds(left, SPAN)] = y + lanes_ref[0, blocks : blocks + 1, pl.ds(left, SPAN)] * x
            tail = (jnp.exp(jnp.minimum(total - cum, 0.0)) * xdt).astype(jnp.bfloat16)
            span_state = jnp.dot(bt_ref[:, here], tail, preferred_element_type=jnp.float32)
            state = span_state if state is None else jnp.exp(total) * state + span_state
        state_ref[:, pl.ds(left, SPAN)] = state


def norm_kernel(count, *refs):
    y_ref, c_ref, cols_ref, lanes_ref, gather_ref = refs[:5]
    parts = refs[5 : 5 + count]
    out_ref = refs[-1]
    blocks = c_ref.shape[0] // SPAN
    for pair in range(TILE // SPAN):
        left = pl.ds(pair * SPAN, SPAN)
        state = sum(
            lanes_ref[0, k + 1 : k + 2, left] * part[:, left].astype(jnp.float32) for k, part in enumerate(parts)
        ).astype(jnp.bfloat16)
        gain = lanes_ref[0, 0:1, left]
        for block in range(blocks):
            here = pl.ds(block * SPAN, SPAN)
            cols = cols_ref[0, here, :]
            cum = halves(spread(cols, 8 + 2 * pair), spread(cols, 9 + 2 * pair))
            carried = jnp.dot(c_ref[here, :], state, preferred_element_type=jnp.float32)
            ssd = y_ref[here, left] + jnp.exp(cum) * carried
            square = ssd * ssd
            high = square.astype(jnp.bfloat16)
            low = (square - high.astype(jnp.float32)).astype(jnp.bfloat16)
            mean = jnp.dot(high, gather_ref[...], preferred_element_type=jnp.float32)
            mean = mean + jnp.dot(low, gather_ref[...], preferred_element_type=jnp.float32)
            out_ref[here, left] = (ssd * lax.rsqrt(mean + 1e-05) * gain).astype(jnp.bfloat16)


def whole(shape):
    return pl.BlockSpec(shape, lambda *_: (0,) * len(shape))


def params():
    return pltpu.CompilerParams(vmem_limit_bytes=VMEM)


def run_bc(tok_ext, w, taps, tok_count, at):
    rows, depth = tok_ext.shape
    blocks = tok_count // SPAN
    return pl.pallas_call(
        bc_kernel,
        grid=(1,),
        in_specs=[
            whole(tok_ext.shape),
            pl.BlockSpec((depth, TILE), lambda i: (0, at)),
            pl.BlockSpec((8, TILE), lambda i: (0, taps.shape[1] // TILE - 1)),
        ],
        out_specs=[whole((tok_count, SPAN)), whole((SPAN, tok_count)), whole((blocks, SPAN, SPAN))],
        out_shape=[
            jax.ShapeDtypeStruct((tok_count, SPAN), jnp.bfloat16),
            jax.ShapeDtypeStruct((SPAN, tok_count), jnp.bfloat16),
            jax.ShapeDtypeStruct((blocks, SPAN, SPAN), jnp.float32),
        ],
        scratch_shapes=[pltpu.VMEM((rows, TILE), jnp.float32)],
        compiler_params=params(),
        cost_estimate=pl.CostEstimate(flops=2 * rows * depth * TILE, bytes_accessed=2 * depth * (rows + TILE), transcendentals=0),
        name="project_bc",
    )(tok_ext, w, taps)


def run_ssd(tok_ext, w, taps, c_rows, b_t, scores, cols, rowsv, lanes, first, tiles, at):
    rows, depth = tok_ext.shape
    tok_count = c_rows.shape[0]
    blocks = scores.shape[0]
    return pl.pallas_call(
        ssd_kernel,
        grid=(tiles,),
        in_specs=[
            whole(tok_ext.shape),
            pl.BlockSpec((depth, TILE), lambda i: (0, i + at)),
            pl.BlockSpec((8, TILE), lambda i: (0, i + first)),
            whole(c_rows.shape),
            whole(b_t.shape),
            whole(scores.shape),
            pl.BlockSpec((1,) + cols.shape[1:], lambda i: (i + first, 0, 0)),
            pl.BlockSpec((1,) + rowsv.shape[1:], lambda i: (i + first, 0, 0)),
            pl.BlockSpec((1,) + lanes.shape[1:], lambda i: (i + first, 0, 0)),
        ],
        out_specs=[
            pl.BlockSpec((tok_count, TILE), lambda i: (0, i)),
            pl.BlockSpec((SPAN, TILE), lambda i: (0, i)),
        ],
        out_shape=[
            jax.ShapeDtypeStruct((tok_count, tiles * TILE), jnp.float32),
            jax.ShapeDtypeStruct((SPAN, tiles * TILE), jnp.float32),
        ],
        scratch_shapes=[pltpu.VMEM((rows, TILE), jnp.float32)],
        compiler_params=params(),
        cost_estimate=pl.CostEstimate(
            flops=6 * rows * depth * TILE * tiles, bytes_accessed=2 * depth * (rows + TILE * tiles), transcendentals=0
        ),
        name="project_ssd",
    )(tok_ext, w, taps, c_rows, b_t, scores, cols, rowsv, lanes)


def run_norm(out, y, c_rows, cols, lanes, gather, parts, first, width):
    tok_count = c_rows.shape[0]
    tiles = y.shape[1] // TILE
    count = len(parts)
    ins = [y, c_rows, cols, lanes, gather, *parts]
    specs = [
        pl.BlockSpec((tok_count, TILE), lambda i: (0, i)),
        whole(c_rows.shape),
        pl.BlockSpec((1,) + cols.shape[1:], lambda i: (i + first, 0, 0)),
        pl.BlockSpec((1,) + lanes.shape[1:], lambda i: (i + first, 0, 0)),
        whole(gather.shape),
    ] + [pl.BlockSpec((SPAN, TILE), lambda i: (0, i))] * count
    aliases = {}
    if out is not None:
        aliases = {len(ins): 0}
        ins.append(out)
        specs.append(pl.BlockSpec(memory_space=pl.ANY))
    return pl.pallas_call(
        lambda *refs: norm_kernel(count, *refs),
        grid=(tiles,),
        in_specs=specs,
        out_specs=pl.BlockSpec((tok_count, TILE), lambda i: (0, i + first)),
        out_shape=jax.ShapeDtypeStruct((tok_count, width), jnp.bfloat16),
        input_output_aliases=aliases,
        compiler_params=params(),
        cost_estimate=pl.CostEstimate(
            flops=6 * tok_count * SPAN * TILE * tiles, bytes_accessed=8 * tok_count * TILE * tiles, transcendentals=0
        ),
        name="head_norm",
    )(*ins)


def shifted(value, z_by, y_by, z_count, y_count):
    pairs = []
    for z in range(z_count - z_by):
        for y in range(y_count):
            pairs.append((z * y_count + y, (z + z_by) * y_count + (y + y_by) % y_count))
    return lax.ppermute(value, "seq", pairs)


def expand(per_head, head_size):
    return jnp.repeat(per_head, head_size, axis=-1)


def local(tokens, w_xbc, conv_weight, conv_bias, a_log, dt_in, d_skip, norm_gain):
    token_rows = tokens[0]
    tok_count = token_rows.shape[0]
    heads = a_log.shape[0]
    width_x = norm_gain.shape[0]
    head_size = width_x // heads
    channels = w_xbc.shape[1]
    blocks = tok_count // SPAN
    tiles = width_x // TILE
    per_tile = TILE // head_size
    seq_count = lax.axis_size("seq")
    z_count = 4
    y_count = seq_count // z_count
    y_mine = lax.rem(lax.axis_index("seq"), y_count)

    w_full = lax.all_gather(w_xbc, ("dp", "seq"), axis=0, tiled=True)
    rim = lax.ppermute(token_rows[tok_count - RIM :], "seq", [(i, i + 1) for i in range(seq_count - 1)])
    tok_ext = jnp.concatenate([rim, token_rows], axis=0)
    taps = jnp.concatenate([conv_weight, conv_bias[None], jnp.zeros((3, channels), jnp.float32)], axis=0)

    step_size = jax.nn.softplus(dt_in[0])
    log_decay = -jnp.exp(a_log)[:, None] * step_size
    cumul = jnp.cumsum(log_decay.reshape(heads, blocks, SPAN), axis=2)
    totals = cumul[:, :, -1]
    before = jnp.cumsum(totals, axis=1) - totals
    cum_full = (cumul + before[:, :, None]).reshape(heads, tok_count)
    own_decay = jnp.sum(totals, axis=1)
    cumul = cumul.reshape(heads, tok_count)
    by_tile = lambda rows: rows.reshape(tiles, per_tile, tok_count)
    cols = jnp.concatenate([by_tile(cumul), by_tile(step_size), by_tile(cum_full)], axis=1).transpose(0, 2, 1)
    rowsv = by_tile(cumul)
    lane_tiles = lambda rows: rows.reshape(rows.shape[0], tiles, TILE).transpose(1, 0, 2)
    lanes = lane_tiles(jnp.concatenate([expand(totals.T, head_size), expand(d_skip[None], head_size), jnp.zeros((1, width_x), jnp.float32)], axis=0))

    side = jnp.broadcast_to(jnp.pad(own_decay, (0, SPAN - heads))[None], (8, SPAN))
    y_decay = [own_decay] + [shifted(side, 0, k, z_count, y_count)[0, :heads] for k in range(1, y_count)]
    y_place = [lax.rem(y_mine - k + y_count, y_count) for k in range(y_count)]
    z_own = jnp.broadcast_to(jnp.pad(sum(y_decay), (0, SPAN - heads))[None], (8, SPAN))
    z_decay = [shifted(z_own, k, 0, z_count, y_count)[0, :heads] for k in range(1, z_count - 1)]
    zero = jnp.zeros_like(own_decay)
    group_coef, own_coef = [], []
    for k in range(y_count):
        after = sum(jnp.where(y_place[m] > y_place[k], y_decay[m], zero) for m in range(y_count))
        until = sum(jnp.where((y_place[m] > y_place[k]) & (y_place[m] < y_mine), y_decay[m], zero) for m in range(y_count))
        group_coef.append(expand(jnp.exp(after), head_size))
        own_coef.append(expand(jnp.where(y_place[k] < y_mine, jnp.exp(until), zero), head_size))
    inside = sum(jnp.where(y_place[m] < y_mine, y_decay[m], zero) for m in range(y_count))
    z_coef = []
    for k in range(1, z_count):
        z_coef.append(expand(jnp.exp(inside + sum(z_decay[: k - 1], zero)), head_size))
    coef_rows = [norm_gain] + own_coef[1:] + z_coef
    coef_rows += [jnp.zeros_like(norm_gain)] * (-len(coef_rows) % 8)
    coefs = lane_tiles(jnp.stack(coef_rows))
    head_of = jnp.arange(SPAN) // head_size
    gather = jnp.where(head_of[:, None] == head_of[None, :], 1.0 / head_size, 0.0).astype(jnp.bfloat16)

    c_rows, b_t, scores = run_bc(tok_ext, w_full, taps, tok_count, tiles)
    cuts = [0, 4, 8, tiles]
    pending = []
    for first, last in zip(cuts[:-1], cuts[1:]):
        y, own = run_ssd(tok_ext, w_full, taps, c_rows, b_t, scores, cols, rowsv, lanes, first, last - first, first)
        lane = slice(first * TILE, last * TILE)
        sent = own.astype(jnp.bfloat16)
        y_parts = [shifted(sent, 0, k, z_count, y_count) for k in range(1, y_count)]
        group = group_coef[0][lane] * own
        for k, part in enumerate(y_parts):
            group = group + group_coef[k + 1][lane] * part.astype(jnp.float32)
        group = group.astype(jnp.bfloat16)
        z_parts = [shifted(group, k, 0, z_count, y_count) for k in range(1, z_count)]
        pending.append((y, y_parts + z_parts, first))
    out = None
    for y, parts, first in pending:
        out = run_norm(out, y, c_rows, cols, coefs, gather, parts, first, width_x)
    return out[None]


def solution(mesh):
    return jax.shard_map(
        local,
        mesh=mesh,
        in_specs=(
            P("dp", "seq", None),
            P(("dp", "seq"), None),
            P(),
            P(),
            P(),
            P("dp", None, "seq"),
            P(),
            P(),
        ),
        out_specs=P("dp", "seq", None),
        check_vma=False,
    )
```

```python
import math

import jax
import jax.numpy as jnp
from jax import lax
from jax.experimental import pallas as pl
from jax.experimental.pallas import tpu as pltpu
from jax.sharding import PartitionSpec as P

SPAN = 128
TILE = 256
RIM = 16
VMEM = 56 * 1024 * 1024
LOG2E = math.log2(math.e)
BF16 = jnp.bfloat16
F32 = jnp.float32


def halves(left, right):
    lane = lax.broadcasted_iota(jnp.int32, left.shape, 1)
    return jnp.where(lane < left.shape[1] // 2, left, right)


def spread(columns, index):
    return jnp.broadcast_to(columns[:, index : index + 1], (columns.shape[0], SPAN))


def convolve(rows_ref, taps_ref, base, left):
    cols = pl.ds(left, SPAN)
    accum = jnp.broadcast_to(taps_ref[4:5, cols], (SPAN, SPAN))
    for tap in range(4):
        accum = accum + taps_ref[tap : tap + 1, cols] * rows_ref[pl.ds(base + RIM - 3 + tap, SPAN), cols]
    half = 0.5 * accum
    return half * jnp.tanh(half) + half


def project(tok_ref, w_ref, rows_ref):
    out = jnp.dot(tok_ref[...], w_ref[...], preferred_element_type=F32)
    rows_ref[...] = out.astype(BF16).astype(F32)


def scores_of(taps_ref, c_ref, bt_ref, scores_ref, rows_ref):
    row = lax.broadcasted_iota(jnp.int32, (SPAN, SPAN), 0)
    col = lax.broadcasted_iota(jnp.int32, (SPAN, SPAN), 1)
    for block in range(scores_ref.shape[0]):
        here = pl.ds(block * SPAN, SPAN)
        b_t = convolve(rows_ref, taps_ref, block * SPAN, 0).astype(BF16).astype(F32).T
        c_rows = convolve(rows_ref, taps_ref, block * SPAN, SPAN).astype(BF16)
        bt_ref[:, here] = b_t
        c_ref[here, :] = c_rows
        scores = jnp.dot(c_rows, b_t.astype(BF16), preferred_element_type=F32)
        scores_ref[block] = jnp.where(row >= col, scores, 0.0)


def scan_tile(taps_ref, c_ref, bt_ref, scores_ref, cols_ref, rowsv_ref, lanes_ref, y_ref, state_ref, rows_ref):
    blocks = scores_ref.shape[0]
    pairs = TILE // SPAN
    states = [None] * pairs
    for block in range(blocks):
        here = pl.ds(block * SPAN, SPAN)
        for pair in range(pairs):
            lanes = pl.ds(pair * SPAN, SPAN)
            cols = cols_ref[0, here, :]
            x = convolve(rows_ref, taps_ref, block * SPAN, pair * SPAN).astype(BF16).astype(F32)
            cums = [spread(cols, 2 * pair), spread(cols, 2 * pair + 1)]
            scores, b_t = scores_ref[block], bt_ref[:, here]
            mix, tails = [], []
            for head, cum in enumerate(cums):
                at = 2 * pair + head
                across, step, tail = (rowsv_ref[0, k + at : k + at + 1, here] for k in (0, 4, 8))
                mix.append((jnp.exp2(jnp.minimum(cum - across, 0.0)) * (scores * step)).astype(BF16))
                tails.append((b_t * tail).astype(BF16))
            zero = jnp.zeros_like(x)
            stacked = jnp.concatenate([halves(x, zero), halves(zero, x)], axis=0).astype(BF16)
            weights = jnp.concatenate([jnp.concatenate(mix, axis=1), jnp.concatenate(tails, axis=1)], axis=0)
            out = jnp.dot(weights, stacked, preferred_element_type=F32)
            y, state = out[:SPAN], out[SPAN:]
            if block > 0:
                carried = jnp.dot(c_ref[here, :], states[pair].astype(BF16), preferred_element_type=F32)
                y = y + jnp.exp2(halves(*cums)) * carried
                state = lanes_ref[0, block : block + 1, lanes] * states[pair] + state
            y_ref[here, lanes] = (y + lanes_ref[0, blocks : blocks + 1, lanes] * x).astype(BF16)
            states[pair] = state
    for pair in range(pairs):
        state_ref[:, pl.ds(pair * SPAN, SPAN)] = states[pair]


def scan_kernel(leads, tiles, piece_count, lead_at, base, *refs):
    offsets = refs[0]
    pieces = refs[1 : 1 + piece_count]
    tok_ref, taps_ref, cols_ref, rowsv_ref, lanes_ref, taps_bc_ref = refs[1 + piece_count : 7 + piece_count]
    rest = refs[7 + piece_count : -5]
    w_a, w_b, rows_a, rows_b, sems = refs[-5:]
    if leads:
        y_ref, state_ref, c_ref, bt_ref, scores_ref = rest
    else:
        c_ref, bt_ref, scores_ref, y_ref, state_ref = rest
    step = pl.program_id(0)
    items = tiles + leads
    w_refs, rows_refs = (w_a, w_b), (rows_a, rows_b)

    def fetch(item, slot):
        column = (item - leads + base) * TILE
        if leads:
            column = jnp.where(item == 0, lead_at, column)
        column = pl.multiple_of(column, TILE)
        index = 0
        rows = w_a.shape[0] // offsets.shape[0]
        for piece in pieces:
            for part in range(piece.shape[0] // rows):
                target = pl.multiple_of(offsets[index], 16)
                pltpu.make_async_copy(
                    piece.at[pl.ds(part * rows, rows), pl.ds(column, TILE)],
                    w_refs[slot].at[pl.ds(target, rows)],
                    sems.at[slot],
                ).start()
                index += 1

    def arrive(slot):
        pltpu.make_async_copy(w_refs[slot], w_refs[slot], sems.at[slot]).wait()

    def multiply(slot):
        project(tok_ref, w_refs[slot], rows_refs[slot])

    def finish(slot):
        scan_tile(taps_ref, c_ref, bt_ref, scores_ref, cols_ref, rowsv_ref, lanes_ref, y_ref, state_ref, rows_refs[slot])

    def lead(slot):
        scores_of(taps_bc_ref, c_ref, bt_ref, scores_ref, rows_refs[slot])

    @pl.when(step == 0)
    def _():
        fetch(0, 0)
        arrive(0)
        if items > 1:
            fetch(1, 1)
        multiply(0)

    if leads and items > 1:

        @pl.when(step == 1)
        def _():
            arrive(1)
            if items > 2:
                fetch(2, 0)
            multiply(1)
            lead(0)

    for slot in (0, 1):
        low = 1 + leads

        @pl.when((step >= low) & (step < items) & (lax.rem(step, 2) == slot))
        def _():
            arrive(slot)

            @pl.when(step + 1 < items)
            def _():
                fetch(step + 1, 1 - slot)

            multiply(slot)
            finish(1 - slot)

    @pl.when(step == items)
    def _():
        finish((items - 1) % 2)


def norm_kernel(count, *refs):
    y_ref, c_ref, cols_ref, lanes_ref, gather_ref = refs[:5]
    parts = refs[5 : 5 + count]
    out_ref = refs[-1]
    pairs = TILE // SPAN
    states = []
    for pair in range(pairs):
        lanes = pl.ds(pair * SPAN, SPAN)
        state = sum(lanes_ref[0, k + 1 : k + 2, lanes] * part[:, lanes].astype(F32) for k, part in enumerate(parts))
        states.append(state.astype(BF16))
    for block in range(c_ref.shape[0] // SPAN):
        here = pl.ds(block * SPAN, SPAN)
        for pair in range(pairs):
            lanes = pl.ds(pair * SPAN, SPAN)
            cols = cols_ref[0, here, :]
            cum = halves(spread(cols, 4 + 2 * pair), spread(cols, 5 + 2 * pair))
            carried = jnp.dot(c_ref[here, :], states[pair], preferred_element_type=F32)
            ssd = y_ref[here, lanes].astype(F32) + jnp.exp2(cum) * carried
            mean = jnp.dot((ssd * ssd).astype(BF16), gather_ref[...], preferred_element_type=F32)
            out_ref[here, lanes] = (ssd * lax.rsqrt(mean + 1e-05) * lanes_ref[0, 0:1, lanes]).astype(BF16)


def whole(shape):
    return pl.BlockSpec(shape, lambda *_: (0,) * len(shape))


def params():
    return pltpu.CompilerParams(vmem_limit_bytes=VMEM)


def run_scan(pieces, offsets, lead_at, base, tok_ext, taps, shared, cols, rowsv, lanes, first, tiles):
    rows, depth = tok_ext.shape
    tok_count = rows - RIM
    blocks = tok_count // SPAN
    leads = 1 if shared is None else 0
    behind = lambda i: jnp.clip(i - 1 - leads, 0, tiles - 1)
    per_tile = lambda array: pl.BlockSpec((1,) + array.shape[1:], lambda i: (behind(i) + first, 0, 0))
    ins = [offsets, *pieces, tok_ext, taps, cols, rowsv, lanes, taps]
    specs = [pl.BlockSpec(memory_space=pltpu.SMEM)]
    specs += [pl.BlockSpec(memory_space=pl.ANY)] * len(pieces)
    specs += [
        whole(tok_ext.shape),
        pl.BlockSpec((8, TILE), lambda i: (0, behind(i) + first)),
        per_tile(cols),
        per_tile(rowsv),
        per_tile(lanes),
        pl.BlockSpec((8, TILE), lambda i: (0, taps.shape[1] // TILE - 1)),
    ]
    out_shape = [
        jax.ShapeDtypeStruct((tok_count, tiles * TILE), BF16),
        jax.ShapeDtypeStruct((SPAN, tiles * TILE), F32),
    ]
    out_specs = [
        pl.BlockSpec((tok_count, TILE), lambda i: (0, behind(i))),
        pl.BlockSpec((SPAN, TILE), lambda i: (0, behind(i))),
    ]
    shared_shape = [
        jax.ShapeDtypeStruct((tok_count, SPAN), BF16),
        jax.ShapeDtypeStruct((SPAN, tok_count), F32),
        jax.ShapeDtypeStruct((blocks, SPAN, SPAN), F32),
    ]
    shared_specs = [whole(each.shape) for each in shared_shape]
    if leads:
        out_shape += shared_shape
        out_specs += shared_specs
    else:
        ins += shared
        specs += shared_specs
    outs = pl.pallas_call(
        lambda *refs: scan_kernel(leads, tiles, len(pieces), lead_at, base, *refs),
        grid=(tiles + leads + 1,),
        in_specs=specs,
        out_specs=out_specs,
        out_shape=out_shape,
        scratch_shapes=[pltpu.VMEM((depth, TILE), BF16)] * 2
        + [pltpu.VMEM((rows, TILE), F32)] * 2
        + [pltpu.SemaphoreType.DMA((2,))],
        compiler_params=params(),
        cost_estimate=pl.CostEstimate(
            flops=4 * rows * depth * TILE * (tiles + leads), bytes_accessed=2 * depth * (rows + TILE * tiles), transcendentals=0
        ),
        name="project_scan",
    )(*ins)
    return outs[0], outs[1], (list(outs[2:]) if leads else shared)


def run_norm(out, y, c_rows, cols, lanes, gather, parts, first, width):
    tok_count = c_rows.shape[0]
    tiles = y.shape[1] // TILE
    count = len(parts)
    ins = [y, c_rows, cols, lanes, gather, *parts]
    specs = [
        pl.BlockSpec((tok_count, TILE), lambda i: (0, i)),
        whole(c_rows.shape),
        pl.BlockSpec((1,) + cols.shape[1:], lambda i: (i + first, 0, 0)),
        pl.BlockSpec((1,) + lanes.shape[1:], lambda i: (i + first, 0, 0)),
        whole(gather.shape),
    ] + [pl.BlockSpec((SPAN, TILE), lambda i: (0, i))] * count
    aliases = {}
    if out is not None:
        aliases = {len(ins): 0}
        ins.append(out)
        specs.append(pl.BlockSpec(memory_space=pl.ANY))
    return pl.pallas_call(
        lambda *refs: norm_kernel(count, *refs),
        grid=(tiles,),
        in_specs=specs,
        out_specs=pl.BlockSpec((tok_count, TILE), lambda i: (0, i + first)),
        out_shape=jax.ShapeDtypeStruct((tok_count, width), BF16),
        input_output_aliases=aliases,
        compiler_params=params(),
        cost_estimate=pl.CostEstimate(
            flops=6 * tok_count * SPAN * TILE * tiles, bytes_accessed=8 * tok_count * TILE * tiles, transcendentals=0
        ),
        name="head_norm",
    )(*ins)


def shifted(value, z_by, y_by, z_count, y_count):
    pairs = []
    for z in range(z_count - z_by):
        for y in range(y_count):
            pairs.append((z * y_count + y, (z + z_by) * y_count + (y + y_by) % y_count))
    return lax.ppermute(value, "seq", pairs)


def expand(per_head, head_size):
    return jnp.repeat(per_head, head_size, axis=-1)


def local(tokens, w_xbc, conv_weight, conv_bias, a_log, dt_in, d_skip, norm_gain):
    token_rows = tokens[0]
    tok_count = token_rows.shape[0]
    heads = a_log.shape[0]
    width_x = norm_gain.shape[0]
    head_size = width_x // heads
    channels = w_xbc.shape[1]
    blocks = tok_count // SPAN
    tiles = width_x // TILE
    per_tile = TILE // head_size
    seq_count = lax.axis_size("seq")
    z_count = 4
    y_count = seq_count // z_count
    y_mine = lax.rem(lax.axis_index("seq"), y_count)

    w_full = lax.all_gather(w_xbc, ("dp", "seq"), axis=0, tiled=True)
    rim = lax.ppermute(token_rows[tok_count - RIM :], "seq", [(i, i + 1) for i in range(seq_count - 1)])
    tok_ext = jnp.concatenate([rim, token_rows], axis=0)
    taps = jnp.concatenate([conv_weight, conv_bias[None], jnp.zeros((3, channels), F32)], axis=0)

    step_size = jax.nn.softplus(dt_in[0])
    log_decay = (-LOG2E * jnp.exp(a_log))[:, None] * step_size
    cumul = jnp.cumsum(log_decay.reshape(heads, blocks, SPAN), axis=2)
    totals = cumul[:, :, -1]
    before = jnp.cumsum(totals, axis=1) - totals
    tail = (jnp.exp2(totals[:, :, None] - cumul) * step_size.reshape(heads, blocks, SPAN)).reshape(heads, tok_count)
    cum_full = (cumul + before[:, :, None]).reshape(heads, tok_count)
    own_decay = jnp.sum(totals, axis=1)
    cumul = cumul.reshape(heads, tok_count)
    by_tile = lambda rows: rows.reshape(tiles, per_tile, tok_count)
    cols = jnp.concatenate([by_tile(cumul), by_tile(cum_full)], axis=1).transpose(0, 2, 1)
    rowsv = jnp.concatenate([by_tile(cumul), by_tile(step_size), by_tile(tail), by_tile(jnp.zeros_like(tail))], axis=1)
    lane_tiles = lambda rows: rows.reshape(rows.shape[0], tiles, TILE).transpose(1, 0, 2)
    lane_rows = [expand(jnp.exp2(totals).T, head_size), expand(d_skip[None], head_size)]
    lane_rows.append(jnp.zeros((-(blocks + 1) % 8, width_x), F32))
    lanes = lane_tiles(jnp.concatenate(lane_rows, axis=0))

    side = jnp.broadcast_to(jnp.pad(own_decay, (0, SPAN - heads))[None], (8, SPAN))
    y_decay = [own_decay] + [shifted(side, 0, k, z_count, y_count)[0, :heads] for k in range(1, y_count)]
    y_place = [lax.rem(y_mine - k + y_count, y_count) for k in range(y_count)]
    z_own = jnp.broadcast_to(jnp.pad(sum(y_decay), (0, SPAN - heads))[None], (8, SPAN))
    z_decay = [shifted(z_own, k, 0, z_count, y_count)[0, :heads] for k in range(1, z_count - 1)]
    zero = jnp.zeros_like(own_decay)
    group_coef, own_coef = [], []
    for k in range(y_count):
        after = sum(jnp.where(y_place[m] > y_place[k], y_decay[m], zero) for m in range(y_count))
        until = sum(jnp.where((y_place[m] > y_place[k]) & (y_place[m] < y_mine), y_decay[m], zero) for m in range(y_count))
        group_coef.append(expand(jnp.exp2(after), head_size))
        own_coef.append(expand(jnp.where(y_place[k] < y_mine, jnp.exp2(until), zero), head_size))
    inside = sum(jnp.where(y_place[m] < y_mine, y_decay[m], zero) for m in range(y_count))
    z_coef = []
    for k in range(1, z_count):
        z_coef.append(expand(jnp.exp2(inside + sum(z_decay[: k - 1], zero)), head_size))
    coef_rows = [norm_gain] + own_coef[1:] + z_coef
    coef_rows += [jnp.zeros_like(norm_gain)] * (-len(coef_rows) % 8)
    coefs = lane_tiles(jnp.stack(coef_rows))
    head_of = jnp.arange(SPAN) // head_size
    gather = jnp.where(head_of[:, None] == head_of[None, :], 1.0 / head_size, 0.0).astype(BF16)

    shared = None
    cuts = [0, 4, 7, tiles]
    offsets = jnp.zeros((1,), jnp.int32)
    pending = []
    for first, last in zip(cuts[:-1], cuts[1:]):
        y, own, shared = run_scan(
            [w_full], offsets, tiles * TILE, first, tok_ext, taps, shared, cols, rowsv, lanes, first, last - first
        )
        lane = slice(first * TILE, last * TILE)
        sent = own.astype(BF16)
        y_parts = [shifted(sent, 0, k, z_count, y_count) for k in range(1, y_count)]
        group = group_coef[0][lane] * own
        for k, part in enumerate(y_parts):
            group = group + group_coef[k + 1][lane] * part.astype(F32)
        group = group.astype(BF16)
        z_parts = [shifted(group, k, 0, z_count, y_count) for k in range(1, z_count)]
        pending.append((y, y_parts + z_parts, first))
    out = None
    for y, parts, first in pending:
        out = run_norm(out, y, shared[0], cols, coefs, gather, parts, first, width_x)
    return out[None]


def solution(mesh):
    return jax.shard_map(
        local,
        mesh=mesh,
        in_specs=(
            P("dp", "seq", None),
            P(("dp", "seq"), None),
            P(),
            P(),
            P(),
            P("dp", None, "seq"),
            P(),
            P(),
        ),
        out_specs=P("dp", "seq", None),
        check_vma=False,
    )
```

```python
import math

import jax
import jax.numpy as jnp
from jax import lax
from jax.experimental import pallas as pl
from jax.experimental.pallas import tpu as pltpu
from jax.sharding import PartitionSpec as P

SPAN = 128
TILE = 256
RIM = 16
VMEM = 56 * 1024 * 1024
LOG2E = math.log2(math.e)
BF16 = jnp.bfloat16
F32 = jnp.float32


def halves(left, right):
    lane = lax.broadcasted_iota(jnp.int32, left.shape, 1)
    return jnp.where(lane < left.shape[1] // 2, left, right)


def spread(columns, index):
    return jnp.broadcast_to(columns[:, index : index + 1], (columns.shape[0], SPAN))


def convolve(rows_ref, taps_ref, base, left):
    cols = pl.ds(left, SPAN)
    accum = jnp.broadcast_to(taps_ref[4:5, cols], (SPAN, SPAN))
    for tap in range(4):
        accum = accum + taps_ref[tap : tap + 1, cols] * rows_ref[pl.ds(base + RIM - 3 + tap, SPAN), cols]
    half = 0.5 * accum
    return half * jnp.tanh(half) + half


def project(tok_ref, w_ref, rows_ref):
    out = jnp.dot(tok_ref[...], w_ref[...], preferred_element_type=F32)
    rows_ref[...] = out.astype(BF16).astype(F32)


def running_sum(row):
    place = lax.broadcasted_iota(jnp.int32, row.shape, 1)
    by = 1
    while by < row.shape[1]:
        row = row + jnp.where(place >= by, pltpu.roll(row, by, 1), 0.0)
        by *= 2
    return row


def decay_kernel(raw_ref, rate_ref, decay_ref, grow_ref, reach_ref, tails_ref):
    pairs = TILE // SPAN
    heads = 2 * pairs
    count = raw_ref.shape[1]
    blocks = count // heads
    raw = raw_ref[0]
    steps = jnp.maximum(raw, 0.0) + jnp.log1p(jnp.exp(-jnp.abs(raw)))
    rows = running_sum(rate_ref[0] * steps)
    totals = rows[:, SPAN - 1 :]
    tails = jnp.exp2(jnp.minimum(totals - rows, 0.0)) * steps
    before = [jnp.zeros((heads, 1), F32)]
    for block in range(blocks - 1):
        before.append(before[-1] + totals[block * heads : (block + 1) * heads])
    padding = jnp.zeros((SPAN - 2 * count, SPAN), F32)
    cols = jnp.concatenate([rows, rows + jnp.concatenate(before, axis=0), padding], axis=0).T
    for block in range(blocks):
        here = pl.ds(block * SPAN, SPAN)
        for pair in range(pairs):
            lanes = pl.ds(pair * SPAN, SPAN)
            first = block * heads + 2 * pair
            cums = [spread(cols, first), spread(cols, first + 1)]
            for head, cum in enumerate(cums):
                at = first + head
                decay = jnp.exp2(jnp.minimum(cum - rows[at : at + 1], 0.0)) * steps[at : at + 1]
                decay_ref[0, pair, here, pl.ds(head * SPAN, SPAN)] = decay.astype(BF16)
                row = block * pairs + pair
                tails_ref[0, row : row + 1, pl.ds(head * SPAN, SPAN)] = tails[at : at + 1]
            grow_ref[here, lanes] = jnp.exp2(halves(*cums)).astype(BF16)
            reach = halves(spread(cols, count + first), spread(cols, count + first + 1))
            reach_ref[here, lanes] = jnp.exp2(reach).astype(BF16)


def scores_of(taps_ref, c_ref, bt_ref, scores_ref, rows_ref):
    row = lax.broadcasted_iota(jnp.int32, (SPAN, SPAN), 0)
    col = lax.broadcasted_iota(jnp.int32, (SPAN, SPAN), 1)
    for block in range(scores_ref.shape[0]):
        here = pl.ds(block * SPAN, SPAN)
        b_t = convolve(rows_ref, taps_ref, block * SPAN, 0).astype(BF16).astype(F32).T
        c_rows = convolve(rows_ref, taps_ref, block * SPAN, SPAN).astype(BF16)
        bt_ref[:, here] = b_t
        c_ref[here, :] = c_rows
        scores = jnp.dot(c_rows, b_t.astype(BF16), preferred_element_type=F32)
        scores = jnp.where(row >= col, scores, 0.0).astype(BF16)
        scores_ref[block] = jnp.concatenate([scores, scores], axis=1)


def scan_tile(taps_ref, c_ref, bt_ref, scores_ref, decay_ref, grow_ref, tails_ref, lanes_ref, y_ref, state_ref, sent_ref, rows_ref):
    blocks = scores_ref.shape[0]
    pairs = TILE // SPAN
    states = [None] * pairs
    for block in range(blocks):
        here = pl.ds(block * SPAN, SPAN)
        for pair in range(pairs):
            lanes = pl.ds(pair * SPAN, SPAN)
            x = convolve(rows_ref, taps_ref, block * SPAN, pair * SPAN).astype(BF16).astype(F32)
            mix = decay_ref[0, pair, here, :] * scores_ref[block]
            b_t = bt_ref[:, here]
            at = block * pairs + pair
            tail = jnp.concatenate([b_t, b_t], axis=1) * tails_ref[0, at : at + 1, :]
            zero = jnp.zeros_like(x)
            stacked = jnp.concatenate([halves(x, zero), halves(zero, x)], axis=0).astype(BF16)
            weights = jnp.concatenate([mix, tail.astype(BF16)], axis=0)
            out = jnp.dot(weights, stacked, preferred_element_type=F32)
            y, state = out[:SPAN], out[SPAN:]
            if block > 0:
                carried = jnp.dot(c_ref[here, :], states[pair].astype(BF16), preferred_element_type=F32)
                y = y + grow_ref[here, lanes].astype(F32) * carried
                state = lanes_ref[0, block : block + 1, lanes] * states[pair] + state
            y_ref[here, lanes] = (y + lanes_ref[0, blocks : blocks + 1, lanes] * x).astype(BF16)
            states[pair] = state
    for pair in range(pairs):
        state_ref[:, pl.ds(pair * SPAN, SPAN)] = states[pair]
        sent_ref[:, pl.ds(pair * SPAN, SPAN)] = states[pair].astype(BF16)


def scan_kernel(leads, tiles, piece_count, lead_at, base, *refs):
    offsets = refs[0]
    pieces = refs[1 : 1 + piece_count]
    rim_ref, tokens_ref, taps_ref, decay_ref, grow_ref, tails_ref, lanes_ref, taps_bc_ref = refs[1 + piece_count : 9 + piece_count]
    rest = refs[9 + piece_count : -6]
    tok_ref, w_a, w_b, rows_a, rows_b, sems = refs[-6:]
    if leads:
        y_ref, state_ref, sent_ref, c_ref, bt_ref, scores_ref = rest
    else:
        c_ref, bt_ref, scores_ref, y_ref, state_ref, sent_ref = rest
    step = pl.program_id(0)
    items = tiles + leads
    w_refs, rows_refs = (w_a, w_b), (rows_a, rows_b)

    def fetch(item, slot):
        column = (item - leads + base) * TILE
        if leads:
            column = jnp.where(item == 0, lead_at, column)
        column = pl.multiple_of(column, TILE)
        index = 0
        rows = w_a.shape[0] // offsets.shape[0]
        for piece in pieces:
            for part in range(piece.shape[0] // rows):
                target = pl.multiple_of(offsets[index], 16)
                pltpu.make_async_copy(
                    piece.at[pl.ds(part * rows, rows), pl.ds(column, TILE)],
                    w_refs[slot].at[pl.ds(target, rows)],
                    sems.at[slot],
                ).start()
                index += 1

    def arrive(slot):
        pltpu.make_async_copy(w_refs[slot], w_refs[slot], sems.at[slot]).wait()

    def multiply(slot):
        project(tok_ref, w_refs[slot], rows_refs[slot])

    def finish(slot):
        scan_tile(
            taps_ref, c_ref, bt_ref, scores_ref, decay_ref, grow_ref, tails_ref, lanes_ref, y_ref, state_ref, sent_ref, rows_refs[slot]
        )

    def lead(slot):
        scores_of(taps_bc_ref, c_ref, bt_ref, scores_ref, rows_refs[slot])

    @pl.when(step == 0)
    def _():
        copies = [
            pltpu.make_async_copy(rim_ref, tok_ref.at[pl.ds(0, RIM)], sems.at[2]),
            pltpu.make_async_copy(tokens_ref, tok_ref.at[pl.ds(RIM, tokens_ref.shape[0])], sems.at[3]),
        ]
        for copy in copies:
            copy.start()
        fetch(0, 0)
        for copy in copies:
            copy.wait()
        arrive(0)
        if items > 1:
            fetch(1, 1)
        multiply(0)

    if leads and items > 1:

        @pl.when(step == 1)
        def _():
            arrive(1)
            if items > 2:
                fetch(2, 0)
            multiply(1)
            lead(0)

    for slot in (0, 1):
        low = 1 + leads

        @pl.when((step >= low) & (step < items) & (lax.rem(step, 2) == slot))
        def _():
            arrive(slot)

            @pl.when(step + 1 < items)
            def _():
                fetch(step + 1, 1 - slot)

            multiply(slot)
            finish(1 - slot)

    @pl.when(step == items)
    def _():
        finish((items - 1) % 2)


def norm_kernel(y_ref, c_ref, reach_ref, gain_ref, gather_ref, state_ref, *rest):
    out_ref = rest[-1]
    carried = jnp.dot(c_ref[...], state_ref[...], preferred_element_type=F32)
    ssd = y_ref[...].astype(F32) + reach_ref[...].astype(F32) * carried
    mean = jnp.dot((ssd * ssd).astype(BF16), gather_ref[...], preferred_element_type=F32)
    out_ref[...] = (ssd * lax.rsqrt(mean + 1e-05) * gain_ref[...]).astype(BF16)


def whole(shape):
    return pl.BlockSpec(shape, lambda *_: (0,) * len(shape))


def params():
    return pltpu.CompilerParams(vmem_limit_bytes=VMEM)


def run_decay(raw, rate):
    tiles, count = raw.shape[:2]
    pairs = TILE // SPAN
    tok_count = count // (2 * pairs) * SPAN
    rounds = pairs * tok_count // SPAN
    tail_rows = rounds + -rounds % 8
    return pl.pallas_call(
        decay_kernel,
        grid=(tiles,),
        in_specs=[
            pl.BlockSpec((1, count, SPAN), lambda i: (i, 0, 0)),
            pl.BlockSpec((1, count, 1), lambda i: (i, 0, 0)),
        ],
        out_specs=[
            pl.BlockSpec((1, pairs, tok_count, 2 * SPAN), lambda i: (i, 0, 0, 0)),
            pl.BlockSpec((tok_count, TILE), lambda i: (0, i)),
            pl.BlockSpec((tok_count, TILE), lambda i: (0, i)),
            pl.BlockSpec((1, tail_rows, 2 * SPAN), lambda i: (i, 0, 0)),
        ],
        out_shape=[
            jax.ShapeDtypeStruct((tiles, pairs, tok_count, 2 * SPAN), BF16),
            jax.ShapeDtypeStruct((tok_count, tiles * TILE), BF16),
            jax.ShapeDtypeStruct((tok_count, tiles * TILE), BF16),
            jax.ShapeDtypeStruct((tiles, tail_rows, 2 * SPAN), F32),
        ],
        compiler_params=params(),
        cost_estimate=pl.CostEstimate(flops=10_000_000_000, bytes_accessed=16_000_000, transcendentals=0),
        name="decays",
    )(raw, rate)


def run_scan(pieces, offsets, lead_at, base, rim, tokens, taps, shared, decay, grow, tails, lanes, first, tiles):
    tok_count, depth = tokens.shape
    rows = tok_count + RIM
    blocks = tok_count // SPAN
    leads = 1 if shared is None else 0
    behind = lambda i: jnp.clip(i - 1 - leads, 0, tiles - 1)
    per_tile = lambda array: pl.BlockSpec((1,) + array.shape[1:], lambda i: (behind(i) + first, 0, 0))
    ins = [offsets, *pieces, rim, tokens, taps, decay, grow, tails, lanes, taps]
    specs = [pl.BlockSpec(memory_space=pltpu.SMEM)]
    specs += [pl.BlockSpec(memory_space=pl.ANY)] * (len(pieces) + 2)
    specs += [
        pl.BlockSpec((8, TILE), lambda i: (0, behind(i) + first)),
        pl.BlockSpec((1,) + decay.shape[1:], lambda i: (behind(i) + first, 0, 0, 0)),
        pl.BlockSpec((tok_count, TILE), lambda i: (0, behind(i) + first)),
        per_tile(tails),
        per_tile(lanes),
        pl.BlockSpec((8, TILE), lambda i: (0, taps.shape[1] // TILE - 1)),
    ]
    out_shape = [
        jax.ShapeDtypeStruct((tok_count, tiles * TILE), BF16),
        jax.ShapeDtypeStruct((SPAN, tiles * TILE), F32),
        jax.ShapeDtypeStruct((SPAN, tiles * TILE), BF16),
    ]
    out_specs = [
        pl.BlockSpec((tok_count, TILE), lambda i: (0, behind(i))),
        pl.BlockSpec((SPAN, TILE), lambda i: (0, behind(i))),
        pl.BlockSpec((SPAN, TILE), lambda i: (0, behind(i))),
    ]
    shared_shape = [
        jax.ShapeDtypeStruct((tok_count, SPAN), BF16),
        jax.ShapeDtypeStruct((SPAN, tok_count), F32),
        jax.ShapeDtypeStruct((blocks, SPAN, 2 * SPAN), BF16),
    ]
    shared_specs = [whole(each.shape) for each in shared_shape]
    if leads:
        out_shape += shared_shape
        out_specs += shared_specs
    else:
        ins += shared
        specs += shared_specs
    outs = pl.pallas_call(
        lambda *refs: scan_kernel(leads, tiles, len(pieces), lead_at, base, *refs),
        grid=(tiles + leads + 1,),
        in_specs=specs,
        out_specs=out_specs,
        out_shape=out_shape,
        scratch_shapes=[pltpu.VMEM((rows, depth), BF16)]
        + [pltpu.VMEM((depth, TILE), BF16)] * 2
        + [pltpu.VMEM((rows, TILE), F32)] * 2
        + [pltpu.SemaphoreType.DMA((4,))],
        compiler_params=params(),
        cost_estimate=pl.CostEstimate(flops=1, bytes_accessed=1, transcendentals=0),
        name="project_scan",
    )(*ins)
    return *outs[:3], (list(outs[3:]) if leads else shared)


def run_norm(out, y, c_rows, reach, gain, gather, state, first, base, tiles, width):
    tok_count = c_rows.shape[0]
    ins = [y, c_rows, reach, gain, gather, state]
    specs = [
        pl.BlockSpec((tok_count, TILE), lambda i: (0, i + base)),
        whole(c_rows.shape),
        pl.BlockSpec((tok_count, TILE), lambda i: (0, i + first)),
        pl.BlockSpec((1, TILE), lambda i: (0, i + first)),
        whole(gather.shape),
        pl.BlockSpec((SPAN, TILE), lambda i: (0, i + base)),
    ]
    aliases = {}
    if out is not None:
        aliases = {len(ins): 0}
        ins.append(out)
        specs.append(pl.BlockSpec(memory_space=pl.ANY))
    return pl.pallas_call(
        norm_kernel,
        grid=(tiles,),
        in_specs=specs,
        out_specs=pl.BlockSpec((tok_count, TILE), lambda i: (0, i + first)),
        out_shape=jax.ShapeDtypeStruct((tok_count, width), BF16),
        input_output_aliases=aliases,
        compiler_params=params(),
        cost_estimate=pl.CostEstimate(flops=400_000_000 * tiles, bytes_accessed=5 * tok_count * TILE * tiles, transcendentals=0),
        name="head_norm",
    )(*ins)


def shifted(value, z_by, y_by, z_count, y_count):
    pairs = []
    for z in range(z_count - z_by):
        for y in range(y_count):
            pairs.append((z * y_count + y, (z + z_by) * y_count + (y + y_by) % y_count))
    return lax.ppermute(value, "seq", pairs)


def stack(*arrays):
    return jnp.concatenate(arrays, axis=0)


def together(*arrays):
    return lax.optimization_barrier(arrays)


class Links:
    def __init__(self, z_count, y_count):
        self.z_count, self.y_count = z_count, y_count

    def index(self, x, core, z, y):
        return (x * 2 + core) * self.z_count * self.y_count + z * self.y_count + y

    def send(self, value, target):
        pairs = []
        for x in range(2):
            for core in range(2):
                for z in range(self.z_count):
                    for y in range(self.y_count):
                        pairs.append((self.index(x, core, z, y), self.index(*target(x, core, z, y))))
        return lax.ppermute(value, ("dp", "seq"), pairs)

    def along_z(self, value, by):
        return self.send(value, lambda x, core, z, y: (x, core, (z + by) % self.z_count, y))

    def first(self, value):
        return self.send(value, lambda x, core, z, y: (x, core, z, 1 - y) if core else (1 - x, core, z, y))

    def second(self, value):
        return self.send(value, lambda x, core, z, y: (1 - x, core, z, y) if core else (x, core, z, 1 - y))

    def sibling(self, value):
        return self.send(value, lambda x, core, z, y: (x, 1 - core, z, y))

    def gather(self, own, early, decays, last):
        z1, z3, own_1, own_2 = together(self.along_z(own, 1), self.along_z(own, 3), self.first(own), self.second(own))
        near = stack(z1, z3)
        z2, near_1, near_2, own_12, *early = together(
            self.along_z(own, 2), self.first(near), self.second(near), self.second(own_1), *early
        )
        mine = stack(own, own_1, own_2, own_12)
        far_1, far_2, near_12, mine_other, *decays = together(
            self.first(z2), self.second(z2), self.second(near_1), self.sibling(mine), *decays(early)
        )
        beside = stack(near, near_1, near_2, near_12)
        far_12, beside_other, *last = together(self.second(far_1), self.sibling(beside), *last(early))
        far = stack(z2, far_1, far_2, far_12)
        return [mine, beside, far, mine_other, beside_other, self.sibling(far)], early, decays, last

    def owners(self):
        dp, seq = lax.axis_index("dp"), lax.axis_index("seq")
        x, core = dp // 2, dp % 2
        z, y = seq // self.y_count, seq % self.y_count
        places = []
        for at in (core, 1 - core):
            for hops in ((0,), (1, 3), (2,)):
                for by_first, by_second in ((0, 0), (1, 0), (0, 1), (1, 1)):
                    for hop in hops:
                        turn_x = jnp.where(at == 0, by_first, by_second)
                        turn_y = jnp.where(at == 0, by_second, by_first)
                        other = (z - hop + self.z_count) % self.z_count
                        places.append(self.index((x + turn_x) % 2, at, other, (y + turn_y) % 2))
        return jnp.stack(places).astype(jnp.int32)


def expand(per_head, head_size):
    return jnp.repeat(per_head, head_size, axis=-1)


def local(tokens, w_xbc, conv_weight, conv_bias, a_log, dt_in, d_skip, norm_gain):
    token_rows = tokens[0]
    tok_count = token_rows.shape[0]
    heads = a_log.shape[0]
    width_x = norm_gain.shape[0]
    head_size = width_x // heads
    channels = w_xbc.shape[1]
    blocks = tok_count // SPAN
    tiles = width_x // TILE
    per_tile = TILE // head_size
    seq_count = lax.axis_size("seq")
    z_count = 4
    y_count = seq_count // z_count
    y_mine = lax.rem(lax.axis_index("seq"), y_count)

    rim = lax.ppermute(token_rows[tok_count - RIM :], "seq", [(i, i + 1) for i in range(seq_count - 1)])
    taps = jnp.concatenate([conv_weight, conv_bias[None], jnp.zeros((3, channels), F32)], axis=0)
    rate = -LOG2E * jnp.exp(a_log)
    totals = rate[:, None] * jnp.sum(jax.nn.softplus(dt_in[0]).reshape(heads, blocks, SPAN), axis=2)
    head_of = jnp.arange(TILE) // head_size
    gather = jnp.where(head_of[:, None] == head_of[None, :], 1.0 / head_size, 0.0).astype(BF16)

    def lane_rows(totals):
        rows = jnp.concatenate([jnp.exp2(totals).T, d_skip[None]], axis=0)
        rows = jnp.pad(expand(rows, head_size), ((0, -(blocks + 1) % 8), (0, 0)))
        return rows.reshape(rows.shape[0], tiles, TILE).transpose(1, 0, 2)

    def along_y(totals):
        own = jnp.sum(totals, axis=1)
        side = jnp.broadcast_to(jnp.pad(own, (0, SPAN - heads))[None], (8, SPAN))
        return [own] + [shifted(side, 0, k, z_count, y_count)[0, :heads] for k in range(1, y_count)]

    def along_z(y_decay):
        own = jnp.broadcast_to(jnp.pad(sum(y_decay), (0, SPAN - heads))[None], (8, SPAN))
        return [shifted(own, k, 0, z_count, y_count)[0, :heads] for k in range(1, z_count - 1)]

    def z_weights(z_decay):
        reach = [jnp.zeros((heads,), F32)]
        for decay in z_decay:
            reach.append(reach[-1] + decay)
        return reach[1:]

    gathered = lambda rows: lax.all_gather(rows, ("dp", "seq"), axis=0, tiled=True)
    whole_rows = jnp.zeros((1,), jnp.int32)
    by_block = lambda rows: rows.reshape(tiles, per_tile, blocks, -1).swapaxes(1, 2).reshape(tiles, blocks * per_tile, -1)
    raw = by_block(dt_in[0])
    rates = by_block(jnp.broadcast_to(rate[:, None], (heads, blocks)))
    lanes = lane_rows(totals)
    if lax.axis_size("dp") == 4 and seq_count == 8:
        split = tiles // 2
        links = Links(z_count, y_count)
        late_w = gathered(w_xbc[:, : split * TILE])
        early_rows = links.owners() * w_xbc.shape[0]

        def coefs(y_decay):
            pair = [jnp.where(y_mine == 0, y_decay[k], y_decay[1 - k]) for k in (0, 1)]
            rows = jnp.stack(pair + z_weights(along_z(y_decay)))
            return [expand(jnp.exp2(rows), head_size)]

        early_w, prepared, (decay, grow, reach, tails), (weights,) = links.gather(
            w_xbc[:, split * TILE :],
            (rim, taps, lanes, gather, early_rows, raw, rates, *along_y(totals)),
            lambda ready: run_decay(*ready[5:7]),
            lambda ready: coefs(ready[7:]),
        )
        rim, taps, lanes, gather, early_rows = prepared[:5]
        calls = [(early_w, early_rows, split, 0, tiles - split), ([late_w], whole_rows, 0, 0, split)]
        lead_at = (tiles - split) * TILE

        def incoming(own, sent, lane):
            e0, e1, z2, z3 = weights[:, lane]
            half = own.shape[1] // 2
            upper = y_mine == 1
            of_mine = lambda value: jnp.where(upper, value[..., half:], value[..., :half])
            of_other = lambda value: jnp.where(upper, value[..., :half], value[..., half:])
            swap = lambda value: shifted(value, 0, 1, z_count, y_count)
            mine = of_mine(own)
            other = swap(of_other(sent)).astype(F32)
            e0, e1, z2, z3 = (of_mine(row) for row in (e0, e1, z2, z3))
            plane = jnp.where(upper, mine + e1 * other, e1 * mine + other).astype(BF16)
            below = [shifted(plane, k, 0, z_count, y_count).astype(F32) for k in range(1, z_count)]
            base = below[0] + z2 * below[1] + z3 * below[2]
            above = e0 * base + jnp.where(upper, other, mine)
            theirs = swap(jnp.where(upper, base, above).astype(BF16))
            ours = jnp.where(upper, above, base).astype(BF16)
            return jnp.where(upper, jnp.concatenate([theirs, ours], axis=1), jnp.concatenate([ours, theirs], axis=1))

    else:
        full = gathered(w_xbc)
        calls = [([full], whole_rows, first, first, min(5, tiles - first)) for first in range(0, tiles, 5)]
        lead_at = tiles * TILE
        decay, grow, reach, tails = run_decay(raw, rates)
        y_decay = along_y(totals)
        z_reach = z_weights(along_z(y_decay))

        def incoming(own, sent, lane):
            place = [lax.rem(y_mine - k + y_count, y_count) for k in range(y_count)]
            spread_lanes = lambda row: expand(row, head_size)[lane]
            inner = lambda keep: sum(jnp.where(keep(m), y_decay[m], 0.0) for m in range(y_count))
            parts = [own] + [shifted(sent, 0, k, z_count, y_count).astype(F32) for k in range(1, y_count)]
            plane, above = 0.0, 0.0
            for k, part in enumerate(parts):
                after = inner(lambda m: place[m] > place[k])
                until = inner(lambda m: (place[m] > place[k]) & (place[m] < y_mine))
                plane = plane + spread_lanes(jnp.exp2(after)) * part
                above = above + spread_lanes(jnp.where(place[k] < y_mine, jnp.exp2(until), 0.0)) * part
            inside = inner(lambda m: place[m] < y_mine)
            plane = plane.astype(BF16)
            for k in range(1, z_count):
                along = inside if k == 1 else inside + z_reach[k - 2]
                above = above + spread_lanes(jnp.exp2(along)) * shifted(plane, k, 0, z_count, y_count).astype(F32)
            return above.astype(BF16)

    shared = None
    pending = []
    for pieces, places, first, base, count in calls:
        y, own, sent, shared = run_scan(
            pieces, places, lead_at, base, rim, token_rows, taps, shared, decay, grow, tails, lanes, first, count
        )
        state = incoming(own, sent, slice(first * TILE, (first + count) * TILE))
        pending.append((y, state, first))
    out = None
    for y, state, first in pending:
        count = y.shape[1] // TILE
        cuts = (0, count // 2, count) if first + count == tiles else (0, count)
        for base, last in zip(cuts[:-1], cuts[1:]):
            out = run_norm(
                out, y, shared[0], reach, norm_gain[None], gather, state, first + base, base, last - base, width_x
            )
    return out[None]


def solution(mesh):
    return jax.shard_map(
        local,
        mesh=mesh,
        in_specs=(
            P("dp", "seq", None),
            P(("dp", "seq"), None),
            P(),
            P(),
            P(),
            P("dp", None, "seq"),
            P(),
            P(),
        ),
        out_specs=P("dp", "seq", None),
        check_vma=False,
    )
```

```python
import math

import jax
import jax.numpy as jnp
from jax import lax
from jax.experimental import pallas as pl
from jax.experimental.pallas import tpu as pltpu
from jax.sharding import PartitionSpec as P

SPAN = 128
TILE = 256
RIM = 16
VMEM = 56 * 1024 * 1024
SMALL = 16 * 1024 * 1024
LOG2E = math.log2(math.e)
BF16 = jnp.bfloat16
F32 = jnp.float32


def halves(left, right):
    lane = lax.broadcasted_iota(jnp.int32, left.shape, 1)
    return jnp.where(lane < left.shape[1] // 2, left, right)


def spread(columns, index):
    return jnp.broadcast_to(columns[:, index : index + 1], (columns.shape[0], SPAN))


def convolve(rows_ref, taps_ref, base, left):
    cols = pl.ds(left, SPAN)
    accum = jnp.broadcast_to(taps_ref[4:5, cols], (SPAN, SPAN))
    for tap in range(4):
        accum = accum + taps_ref[tap : tap + 1, cols] * rows_ref[pl.ds(base + RIM - 3 + tap, SPAN), cols]
    half = 0.5 * accum
    return half * jnp.tanh(half) + half


def project(tok_ref, w_ref, rows_ref):
    out = jnp.dot(tok_ref[...], w_ref[...], preferred_element_type=F32)
    rows_ref[...] = out.astype(BF16).astype(F32)


def running_sum(row):
    place = lax.broadcasted_iota(jnp.int32, row.shape, 1)
    by = 1
    while by < row.shape[1]:
        row = row + jnp.where(place >= by, pltpu.roll(row, by, 1), 0.0)
        by *= 2
    return row


def decay_kernel(raw_ref, rate_ref, decay_ref, grow_ref, reach_ref, tails_ref, steps_ref, rows_ref, tail_ref, cols_ref):
    pairs = TILE // SPAN
    heads = 2 * pairs
    tiles = cols_ref.shape[0]
    count = raw_ref.shape[0] // tiles
    blocks = count // heads
    tile = pl.program_id(0)

    @pl.when(tile == 0)
    def _():
        raw = raw_ref[...]
        steps = jnp.maximum(raw, 0.0) + jnp.log1p(jnp.exp(-jnp.abs(raw)))
        rows = running_sum(rate_ref[...] * steps)
        totals = jnp.broadcast_to(rows[:, SPAN - 1 :], rows.shape)
        steps_ref[...] = steps
        rows_ref[...] = rows
        tail_ref[...] = jnp.exp2(jnp.minimum(totals - rows, 0.0)) * steps
        block = lax.rem(lax.broadcasted_iota(jnp.int32, rows.shape, 0), count) // heads
        before = jnp.where(block >= 1, pltpu.roll(totals, heads, 0), 0.0)
        by = 1
        while by < blocks:
            before = before + jnp.where(block >= by, pltpu.roll(before, by * heads, 0), 0.0)
            by *= 2
        full = rows + before
        padding = jnp.zeros((SPAN - 2 * count, SPAN), F32)
        for each in range(tiles):
            mine = slice(each * count, (each + 1) * count)
            cols_ref[each] = jnp.concatenate([rows[mine], full[mine], padding], axis=0).T

    mine = pl.ds(pl.multiple_of(tile * count, 8), count)
    cols = cols_ref[tile]
    rows, steps, tails = rows_ref[mine, :], steps_ref[mine, :], tail_ref[mine, :]
    for block in range(blocks):
        here = pl.ds(block * SPAN, SPAN)
        for pair in range(pairs):
            lanes = pl.ds(pair * SPAN, SPAN)
            first = block * heads + 2 * pair
            cums = [spread(cols, first), spread(cols, first + 1)]
            for head, cum in enumerate(cums):
                at = first + head
                decay = jnp.exp2(jnp.minimum(cum - rows[at : at + 1], 0.0)) * steps[at : at + 1]
                decay_ref[0, pair, here, pl.ds(head * SPAN, SPAN)] = decay.astype(BF16)
                row = block * pairs + pair
                tails_ref[0, row : row + 1, pl.ds(head * SPAN, SPAN)] = tails[at : at + 1]
            grow_ref[0, here, lanes] = jnp.exp2(halves(*cums)).astype(BF16)
            reach = halves(spread(cols, count + first), spread(cols, count + first + 1))
            reach_ref[0, here, lanes] = jnp.exp2(reach).astype(BF16)


def scores_of(taps_ref, c_ref, bt_ref, scores_ref, rows_ref):
    row = lax.broadcasted_iota(jnp.int32, (SPAN, SPAN), 0)
    col = lax.broadcasted_iota(jnp.int32, (SPAN, SPAN), 1)
    for block in range(scores_ref.shape[0]):
        here = pl.ds(block * SPAN, SPAN)
        b_t = convolve(rows_ref, taps_ref, block * SPAN, 0).astype(BF16).astype(F32).T
        c_rows = convolve(rows_ref, taps_ref, block * SPAN, SPAN).astype(BF16)
        bt_ref[:, here] = b_t
        c_ref[here, :] = c_rows
        scores = jnp.dot(c_rows, b_t.astype(BF16), preferred_element_type=F32)
        scores = jnp.where(row >= col, scores, 0.0).astype(BF16)
        scores_ref[block] = jnp.concatenate([scores, scores], axis=1)


def scan_tile(taps_ref, c_ref, bt_ref, scores_ref, decay_ref, grow_ref, tails_ref, lanes_ref, y_ref, state_ref, sent_ref, rows_ref, upper, extra_ref):
    blocks = scores_ref.shape[0]
    pairs = TILE // SPAN
    states = [None] * pairs
    for block in range(blocks):
        here = pl.ds(block * SPAN, SPAN)
        for pair in range(pairs):
            lanes = pl.ds(pair * SPAN, SPAN)
            x = convolve(rows_ref, taps_ref, block * SPAN, pair * SPAN).astype(BF16).astype(F32)
            mix = decay_ref[0, pair, here, :] * scores_ref[block]
            b_t = bt_ref[:, here]
            at = block * pairs + pair
            tail = jnp.concatenate([b_t, b_t], axis=1) * tails_ref[0, at : at + 1, :]
            zero = jnp.zeros_like(x)
            stacked = jnp.concatenate([halves(x, zero), halves(zero, x)], axis=0).astype(BF16)
            weights = jnp.concatenate([mix, tail.astype(BF16)], axis=0)
            out = jnp.dot(weights, stacked, preferred_element_type=F32)
            y, state = out[:SPAN], out[SPAN:]
            if block > 0:
                carried = jnp.dot(c_ref[here, :], states[pair].astype(BF16), preferred_element_type=F32)
                y = y + grow_ref[0, here, lanes].astype(F32) * carried
                state = lanes_ref[0, block : block + 1, lanes] * states[pair] + state
            y_ref[0, here, lanes] = (y + lanes_ref[0, blocks : blocks + 1, lanes] * x).astype(BF16)
            states[pair] = state
    for pair in range(pairs):
        lanes = pl.ds(pair * SPAN, SPAN)
        if upper is None:
            state_ref[:, lanes] = states[pair]
            sent_ref[:, lanes] = states[pair].astype(BF16)
            continue
        half = SPAN // 2
        low, high = states[pair][:half], states[pair][half:]
        state_ref[:, lanes] = jnp.where(upper, high, low)
        sent_ref[:half, lanes] = jnp.where(upper, low, high).astype(BF16)
    if extra_ref is not None:
        sent_ref[SPAN // 2 :, :] = extra_ref[...]


def scan_kernel(leads, extras, tiles, piece_count, lead_at, base, *refs):
    offsets, place = refs[:2]
    refs = refs[1:]
    pieces = refs[1 : 1 + piece_count]
    rim_ref, tokens_ref, taps_ref, decay_ref, grow_ref, tails_ref, lanes_ref, taps_bc_ref = refs[1 + piece_count : 9 + piece_count]
    rest = refs[9 + piece_count : -6]
    tok_ref, w_a, w_b, rows_a, rows_b, sems = refs[-6:]
    extra_ref = None
    if extras:
        extra_ref, *rest = rest
    if leads:
        y_ref, state_ref, sent_ref, c_ref, bt_ref, scores_ref = rest
    else:
        c_ref, bt_ref, scores_ref, y_ref, state_ref, sent_ref = rest
    step = pl.program_id(0)
    items = tiles + leads
    w_refs, rows_refs = (w_a, w_b), (rows_a, rows_b)

    def fetch(item, slot):
        tile = item - leads + base
        if leads:
            tile = jnp.where(item == 0, lead_at, tile)
        index = 0
        for piece in pieces:
            rows = piece.shape[2]
            for part in range(piece.shape[0]):
                target = pl.multiple_of(offsets[index], 16)
                pltpu.make_async_copy(
                    piece.at[part, tile], w_refs[slot].at[pl.ds(target, rows)], sems.at[slot]
                ).start()
                index += 1

    def arrive(slot):
        pltpu.make_async_copy(w_refs[slot], w_refs[slot], sems.at[slot]).wait()

    def multiply(slot):
        project(tok_ref, w_refs[slot], rows_refs[slot])

    def finish(slot):
        scan_tile(
            taps_ref, c_ref, bt_ref, scores_ref, decay_ref, grow_ref, tails_ref, lanes_ref, y_ref, state_ref, sent_ref, rows_refs[slot],
            place[0] == 1 if state_ref.shape[0] < SPAN else None,
            extra_ref,
        )

    def lead(slot):
        scores_of(taps_bc_ref, c_ref, bt_ref, scores_ref, rows_refs[slot])

    @pl.when(step == 0)
    def _():
        copies = [
            pltpu.make_async_copy(rim_ref, tok_ref.at[pl.ds(0, RIM)], sems.at[2]),
            pltpu.make_async_copy(tokens_ref, tok_ref.at[pl.ds(RIM, tokens_ref.shape[0])], sems.at[3]),
        ]
        for copy in copies:
            copy.start()
        fetch(0, 0)
        for copy in copies:
            copy.wait()
        arrive(0)
        if items > 1:
            fetch(1, 1)
        multiply(0)

    if leads and items > 1:

        @pl.when(step == 1)
        def _():
            arrive(1)
            if items > 2:
                fetch(2, 0)
            multiply(1)
            lead(0)

    for slot in (0, 1):
        low = 1 + leads

        @pl.when((step >= low) & (step < items) & (lax.rem(step, 2) == slot))
        def _():
            arrive(slot)

            @pl.when(step + 1 < items)
            def _():
                fetch(step + 1, 1 - slot)

            multiply(slot)
            finish(1 - slot)

    @pl.when(step == items)
    def _():
        finish((items - 1) % 2)


def norm_kernel(count, place_ref, y_ref, c_ref, reach_ref, gain_ref, gather_ref, *rest):
    out_ref = rest[-1]
    state = rest[0][...]
    if count == 2:
        ours, theirs = state, rest[1][...]
        upper = place_ref[0] == 1
        low, high = jnp.where(upper, theirs, ours), jnp.where(upper, ours, theirs)
        state = jnp.concatenate([low, high], axis=0)
    carried = jnp.dot(c_ref[...], state, preferred_element_type=F32)
    ssd = y_ref[0].astype(F32) + reach_ref[0].astype(F32) * carried
    mean = jnp.dot((ssd * ssd).astype(BF16), gather_ref[...], preferred_element_type=F32)
    out_ref[...] = (ssd * lax.rsqrt(mean + 1e-05) * gain_ref[...]).astype(BF16)


def whole(shape):
    return pl.BlockSpec(shape, lambda *_: (0,) * len(shape))


def params(limit=VMEM):
    return pltpu.CompilerParams(vmem_limit_bytes=limit)


def run_decay(raw, rate):
    tiles, count = raw.shape[:2]
    pairs = TILE // SPAN
    table = pltpu.VMEM((tiles * count, SPAN), F32)
    tok_count = count // (2 * pairs) * SPAN
    rounds = pairs * tok_count // SPAN
    tail_rows = rounds + -rounds % 8
    return pl.pallas_call(
        decay_kernel,
        grid=(tiles,),
        in_specs=[
            whole((tiles * count, SPAN)),
            whole((tiles * count, 1)),
        ],
        out_specs=[
            pl.BlockSpec((1, pairs, tok_count, 2 * SPAN), lambda i: (i, 0, 0, 0)),
            pl.BlockSpec((1, tok_count, TILE), lambda i: (i, 0, 0)),
            pl.BlockSpec((1, tok_count, TILE), lambda i: (i, 0, 0)),
            pl.BlockSpec((1, tail_rows, 2 * SPAN), lambda i: (i, 0, 0)),
        ],
        out_shape=[
            jax.ShapeDtypeStruct((tiles, pairs, tok_count, 2 * SPAN), BF16),
            jax.ShapeDtypeStruct((tiles, tok_count, TILE), BF16),
            jax.ShapeDtypeStruct((tiles, tok_count, TILE), BF16),
            jax.ShapeDtypeStruct((tiles, tail_rows, 2 * SPAN), F32),
        ],
        scratch_shapes=[table, table, table, pltpu.VMEM((tiles, SPAN, SPAN), F32)],
        compiler_params=params(),
        cost_estimate=pl.CostEstimate(flops=10_000_000_000, bytes_accessed=16_000_000, transcendentals=0),
        name="decays",
    )(raw.reshape(tiles * count, SPAN), rate.reshape(tiles * count, 1))


def run_scan(pieces, offsets, place, lead_at, base, rim, tokens, taps, shared, decay, grow, tails, lanes, first, tiles, extra=None):
    tok_count, depth = tokens.shape
    rows = tok_count + RIM
    blocks = tok_count // SPAN
    leads = 1 if shared is None else 0
    behind = lambda i: jnp.clip(i - 1 - leads, 0, tiles - 1)
    per_tile = lambda array: pl.BlockSpec((1,) + array.shape[1:], lambda i: (behind(i) + first, 0, 0))
    held = SPAN // 2 if place is not None else SPAN
    place = jnp.zeros((1,), jnp.int32) if place is None else place
    ins = [offsets, place, *pieces, rim, tokens, taps, decay, grow, tails, lanes, taps]
    specs = [pl.BlockSpec(memory_space=pltpu.SMEM)] * 2
    specs += [pl.BlockSpec(memory_space=pl.ANY)] * (len(pieces) + 2)
    specs += [
        pl.BlockSpec((8, TILE), lambda i: (0, behind(i) + first)),
        pl.BlockSpec((1,) + decay.shape[1:], lambda i: (behind(i) + first, 0, 0, 0)),
        per_tile(grow),
        per_tile(tails),
        per_tile(lanes),
        pl.BlockSpec((8, TILE), lambda i: (0, taps.shape[1] // TILE - 1)),
    ]
    out_shape = [
        jax.ShapeDtypeStruct((tiles, tok_count, TILE), BF16),
        jax.ShapeDtypeStruct((held, tiles * TILE), F32),
        jax.ShapeDtypeStruct((held + (0 if extra is None else extra.shape[0]), tiles * TILE), BF16),
    ]
    out_specs = [
        pl.BlockSpec((1, tok_count, TILE), lambda i: (behind(i), 0, 0)),
        pl.BlockSpec((held, TILE), lambda i: (0, behind(i))),
        pl.BlockSpec((out_shape[2].shape[0], TILE), lambda i: (0, behind(i))),
    ]
    shared_shape = [
        jax.ShapeDtypeStruct((tok_count, SPAN), BF16),
        jax.ShapeDtypeStruct((SPAN, tok_count), F32),
        jax.ShapeDtypeStruct((blocks, SPAN, 2 * SPAN), BF16),
    ]
    shared_specs = [whole(each.shape) for each in shared_shape]
    extras = 0 if extra is None else extra.shape[0]
    if extras:
        ins.append(extra)
        specs.append(pl.BlockSpec((extras, TILE), lambda i: (0, behind(i))))
    if leads:
        out_shape += shared_shape
        out_specs += shared_specs
    else:
        ins += shared
        specs += shared_specs
    outs = pl.pallas_call(
        lambda *refs: scan_kernel(leads, extras, tiles, len(pieces), lead_at, base, *refs),
        grid=(tiles + leads + 1,),
        in_specs=specs,
        out_specs=out_specs,
        out_shape=out_shape,
        scratch_shapes=[pltpu.VMEM((rows, depth), BF16)]
        + [pltpu.VMEM((depth, TILE), BF16)] * 2
        + [pltpu.VMEM((rows, TILE), F32)] * 2
        + [pltpu.SemaphoreType.DMA((4,))],
        compiler_params=params(),
        cost_estimate=pl.CostEstimate(flops=3_000_000_000 * tiles, bytes_accessed=3_000_000 * tiles, transcendentals=0),
        name="project_scan",
    )(*ins)
    return *outs[:3], (list(outs[3:]) if leads else shared)


def run_norm(out, place, y, c_rows, reach, gain, gather, state, first, base, tiles, width):
    tok_count = c_rows.shape[0]
    ins = [place, y, c_rows, reach, gain, gather, *state]
    specs = [
        pl.BlockSpec(memory_space=pltpu.SMEM),
        pl.BlockSpec((1, tok_count, TILE), lambda i: (i + base, 0, 0)),
        whole(c_rows.shape),
        pl.BlockSpec((1, tok_count, TILE), lambda i: (i + first, 0, 0)),
        pl.BlockSpec((1, TILE), lambda i: (0, i + first)),
        whole(gather.shape),
    ]
    specs += [pl.BlockSpec((part.shape[0], TILE), lambda i: (0, i + base)) for part in state]
    aliases = {}
    if out is not None:
        aliases = {len(ins): 0}
        ins.append(out)
        specs.append(pl.BlockSpec(memory_space=pl.ANY))
    return pl.pallas_call(
        lambda *refs: norm_kernel(len(state), *refs),
        grid=(tiles,),
        in_specs=specs,
        out_specs=pl.BlockSpec((tok_count, TILE), lambda i: (0, i + first)),
        out_shape=jax.ShapeDtypeStruct((tok_count, width), BF16),
        input_output_aliases=aliases,
        compiler_params=params(SMALL),
        cost_estimate=pl.CostEstimate(flops=400_000_000 * tiles, bytes_accessed=5 * tok_count * TILE * tiles, transcendentals=0),
        name="head_norm",
    )(*ins)


def shifted(value, z_by, y_by, z_count, y_count):
    pairs = []
    for z in range(z_count - z_by):
        for y in range(y_count):
            pairs.append((z * y_count + y, (z + z_by) * y_count + (y + y_by) % y_count))
    return lax.ppermute(value, "seq", pairs)


def stack(*arrays):
    return jnp.concatenate(arrays, axis=0)


def together(*arrays):
    return lax.optimization_barrier(arrays)


class Links:
    def __init__(self, z_count, y_count):
        self.z_count, self.y_count = z_count, y_count

    def index(self, x, core, z, y):
        return (x * 2 + core) * self.z_count * self.y_count + z * self.y_count + y

    def send(self, value, target):
        pairs = []
        for x in range(2):
            for core in range(2):
                for z in range(self.z_count):
                    for y in range(self.y_count):
                        pairs.append((self.index(x, core, z, y), self.index(*target(x, core, z, y))))
        return lax.ppermute(value, ("dp", "seq"), pairs)

    def along_z(self, value, by):
        return self.send(value, lambda x, core, z, y: (x, core, (z + by) % self.z_count, y))

    def first(self, value):
        return self.send(value, lambda x, core, z, y: (x, core, z, 1 - y) if core else (1 - x, core, z, y))

    def second(self, value):
        return self.send(value, lambda x, core, z, y: (1 - x, core, z, y) if core else (x, core, z, 1 - y))

    def sibling(self, value):
        return self.send(value, lambda x, core, z, y: (x, 1 - core, z, y))

    def gather(self, own, early, decays):
        z1, z3, own_1, own_2, own = together(
            self.along_z(own, 1), self.along_z(own, 3), self.first(own), self.second(own), own
        )
        near = stack(z1, z3)
        z2, near_1, near_2, own_12, *early = together(
            self.along_z(own, 2), self.first(near), self.second(near), self.second(own_1), *early
        )
        mine = stack(own, own_1, own_2, own_12)
        far_1, far_2, near_12, mine_other, *decays = together(
            self.first(z2), self.second(z2), self.second(near_1), self.sibling(mine), *decays(early)
        )
        beside = stack(near, near_1, near_2, near_12)
        far = stack(z2, far_1, far_2)
        far_12, beside_other, far_other = together(self.second(far_1), self.sibling(beside), self.sibling(far))
        return [mine, beside, far, far_12, mine_other, beside_other, far_other, self.sibling(far_12)], early, decays

    def owners(self):
        dp, seq = lax.axis_index("dp"), lax.axis_index("seq")
        x, core = dp // 2, dp % 2
        z, y = seq // self.y_count, seq % self.y_count
        places = []
        for at in (core, 1 - core):
            for hops in ((0,), (1, 3), (2,)):
                for by_first, by_second in ((0, 0), (1, 0), (0, 1), (1, 1)):
                    for hop in hops:
                        turn_x = jnp.where(at == 0, by_first, by_second)
                        turn_y = jnp.where(at == 0, by_second, by_first)
                        other = (z - hop + self.z_count) % self.z_count
                        places.append(self.index((x + turn_x) % 2, at, other, (y + turn_y) % 2))
        return jnp.stack(places).astype(jnp.int32)


def expand(per_head, head_size):
    return jnp.repeat(per_head, head_size, axis=-1)


def local(tokens, w_xbc, conv_weight, conv_bias, a_log, dt_in, d_skip, norm_gain):
    token_rows = tokens[0]
    tok_count = token_rows.shape[0]
    heads = a_log.shape[0]
    width_x = norm_gain.shape[0]
    head_size = width_x // heads
    channels = w_xbc.shape[1]
    blocks = tok_count // SPAN
    tiles = width_x // TILE
    per_tile = TILE // head_size
    seq_count = lax.axis_size("seq")
    z_count = 4
    y_count = seq_count // z_count
    y_mine = lax.rem(lax.axis_index("seq"), y_count)

    after = lambda rows: lax.ppermute(rows, "seq", [(i, i + 1) for i in range(seq_count - 1)])
    rim_rows = token_rows[tok_count - RIM :]
    taps = jnp.concatenate([conv_weight, conv_bias[None], jnp.zeros((3, channels), F32)], axis=0)
    rate = -LOG2E * jnp.exp(a_log)
    totals = rate[:, None] * jnp.sum(jax.nn.softplus(dt_in[0]).reshape(heads, blocks, SPAN), axis=2)
    head_of = jnp.arange(TILE) // head_size
    gather = jnp.where(head_of[:, None] == head_of[None, :], 1.0 / head_size, 0.0).astype(BF16)

    def lane_rows(totals):
        rows = jnp.concatenate([jnp.exp2(totals).T, d_skip[None]], axis=0)
        rows = jnp.pad(expand(rows, head_size), ((0, -(blocks + 1) % 8), (0, 0)))
        return rows.reshape(rows.shape[0], tiles, TILE).transpose(1, 0, 2)

    def along_y(totals):
        own = jnp.sum(totals, axis=1)
        side = jnp.broadcast_to(jnp.pad(own, (0, SPAN - heads))[None], (8, SPAN))
        return [own] + [shifted(side, 0, k, z_count, y_count)[0, :heads] for k in range(1, y_count)]

    def along_z(y_decay):
        own = jnp.broadcast_to(jnp.pad(sum(y_decay), (0, SPAN - heads))[None], (8, SPAN))
        return [shifted(own, k, 0, z_count, y_count)[0, :heads] for k in range(1, z_count - 1)]

    def z_weights(z_decay):
        reach = [jnp.zeros((heads,), F32)]
        for decay in z_decay:
            reach.append(reach[-1] + decay)
        return reach[1:]

    by_block = lambda rows: rows.reshape(tiles, per_tile, blocks, -1).swapaxes(1, 2).reshape(tiles, blocks * per_tile, -1)
    raw = by_block(dt_in[0])
    rates = by_block(jnp.broadcast_to(rate[:, None], (heads, blocks)))
    lanes = lane_rows(totals)
    if lax.axis_size("dp") == 4 and seq_count == 8:
        split = tiles // 2
        links = Links(z_count, y_count)
        row_count = w_xbc.shape[0]
        by_column = w_xbc.reshape(row_count, channels // TILE, TILE).swapaxes(0, 1)[None]
        late_w = lax.all_gather(by_column[:, :split], ("dp", "seq"), axis=0, tiled=True)
        late_rows = jnp.arange(lax.axis_size("dp") * seq_count, dtype=jnp.int32) * row_count
        early_rows = links.owners() * row_count

        kept = expand(jnp.exp2(jnp.sum(totals, axis=1)), head_size)
        wide = (tiles - split) * TILE
        rest = jnp.pad(kept[: split * TILE], (0, -(split * TILE) % wide)).reshape(-1, wide)
        own_kept = jnp.concatenate([kept[None, split * TILE :], rest], axis=0)
        extra = jnp.pad(own_kept, ((0, 16 - own_kept.shape[0]), (0, 0))).astype(BF16)

        early_w, prepared, (decay, grow, reach, tails) = links.gather(
            by_column[:, split:],
            (taps, lanes, gather, early_rows, late_rows, after(rim_rows), own_kept, extra, raw, rates),
            lambda ready: run_decay(*ready[8:]),
        )
        taps, lanes, gather, early_rows, late_rows, rim, own_kept, extra = prepared[:8]
        calls = [(early_w, early_rows, split, 0, tiles - split), ([late_w], late_rows, 0, 0, split)]
        lead_at = tiles - split
        halved = y_mine.astype(jnp.int32)[None]

        upper = y_mine == 1
        swap = lambda value: shifted(value, 0, 1, z_count, y_count)

        half = SPAN // 2

        def plane_of(own, other, upper_kept, rows=None):
            other = other[:half].astype(F32)
            plane = jnp.where(upper, own + upper_kept * other, upper_kept * own + other)
            if rows is not None:
                plane = jnp.concatenate([plane, jnp.pad(rows, ((0, 16 - rows.shape[0]), (0, 0)))], axis=0)
            plane = plane.astype(BF16)
            return [shifted(plane, k, 0, z_count, y_count) for k in range(1, z_count)]

        def halves_of(own, other, below, lower_kept, z_kept):
            base = below[0][:half].astype(F32)
            through = 1.0
            for kept, part in zip(z_kept, below[1:]):
                through = through * kept
                base = base + through * part[:half].astype(F32)
            above = lower_kept * base + jnp.where(upper, other[:half].astype(F32), own)
            theirs = swap(jnp.where(upper, base, above).astype(BF16))
            return [jnp.where(upper, above, base).astype(BF16), theirs]

    else:
        full = lax.all_gather(w_xbc, ("dp", "seq"), axis=0, tiled=True)
        full = full.reshape(full.shape[0], channels // TILE, TILE).swapaxes(0, 1)[None]
        first_row = jnp.zeros((1,), jnp.int32)
        calls = [([full], first_row, first, first, min(5, tiles - first)) for first in range(0, tiles, 5)]
        lead_at = tiles
        rim = after(rim_rows)
        halved = None
        decay, grow, reach, tails = run_decay(raw, rates)
        y_decay = along_y(totals)
        z_reach = z_weights(along_z(y_decay))

        def beside(sent):
            return [shifted(sent, 0, k, z_count, y_count) for k in range(1, y_count)]

        def incoming(own, parts, lane):
            place = [lax.rem(y_mine - k + y_count, y_count) for k in range(y_count)]
            spread_lanes = lambda row: expand(row, head_size)[lane]
            inner = lambda keep: sum(jnp.where(keep(m), y_decay[m], 0.0) for m in range(y_count))
            parts = [own] + [part.astype(F32) for part in parts]
            plane, above = 0.0, 0.0
            for k, part in enumerate(parts):
                after = inner(lambda m: place[m] > place[k])
                until = inner(lambda m: (place[m] > place[k]) & (place[m] < y_mine))
                plane = plane + spread_lanes(jnp.exp2(after)) * part
                above = above + spread_lanes(jnp.where(place[k] < y_mine, jnp.exp2(until), 0.0)) * part
            inside = inner(lambda m: place[m] < y_mine)
            plane = plane.astype(BF16)
            for k in range(1, z_count):
                along = inside if k == 1 else inside + z_reach[k - 2]
                above = above + spread_lanes(jnp.exp2(along)) * shifted(plane, k, 0, z_count, y_count).astype(F32)
            return [above.astype(BF16)]

    def scan(call, shared, extra=None):
        pieces, places, first, base, count = call
        return run_scan(
            pieces, places, halved, lead_at, base, rim, token_rows, taps, shared, decay, grow, tails, lanes, first, count, extra
        )

    def norm(out, y, state, first, base, count):
        place = y_mine.astype(jnp.int32)[None]
        return run_norm(
            out, place, y, shared[0], reach, norm_gain[None], gather, state, first + base, base, count, width_x
        )

    if halved is None:
        shared, out = None, None
        pending = []
        for call in calls:
            y, own, sent, shared = scan(call, shared)
            first, count = call[2], call[4]
            pending.append((y, incoming(own, beside(sent), slice(first * TILE, (first + count) * TILE)), first, 0, count))
        for each in pending:
            out = norm(out, *each)
        return out[None]

    (_, _, first_a, _, count_a), (_, _, first_b, _, count_b) = calls
    y_a, own_a, sent_a, shared = scan(calls[0], None, extra)
    other_a = swap(sent_a)
    kept_rows = slice(half, half + own_kept.shape[0])
    later = lambda rows: rows[1:].reshape(-1)[: count_b * TILE]
    other_kept = other_a[kept_rows].astype(F32)
    lower_kept = jnp.where(upper, other_kept, own_kept)
    upper_kept = jnp.where(upper, own_kept, other_kept)
    pieces, other_a = together(calls[1][0], other_a)
    below_a = plane_of(own_a, other_a, upper_kept[0], lower_kept * upper_kept)
    y_b, own_b, sent_b, _ = scan((pieces, *calls[1][1:]), shared)
    sent_b, *below_a = together(sent_b, *below_a)
    other_b = swap(sent_b)
    z_kept = [part[kept_rows].astype(F32) for part in below_a]
    state_a = halves_of(own_a, other_a, below_a, lower_kept[0], [kept[0] for kept in z_kept])
    below_b = plane_of(own_b, other_b, later(upper_kept))
    out = norm(None, y_a, state_a, first_a, 0, count_a // 2)
    out = norm(out, y_a, state_a, first_a, count_a // 2, count_a - count_a // 2)
    out, *below_b = together(out, *below_b)
    state_b = halves_of(own_b, other_b, below_b, later(lower_kept), [later(kept) for kept in z_kept])
    out = norm(out, y_b, state_b, first_b, 0, count_b)
    return out[None]


def solution(mesh):
    return jax.shard_map(
        local,
        mesh=mesh,
        in_specs=(
            P("dp", "seq", None),
            P(("dp", "seq"), None),
            P(),
            P(),
            P(),
            P("dp", None, "seq"),
            P(),
            P(),
        ),
        out_specs=P("dp", "seq", None),
        check_vma=False,
    )
```

```python
import math

import jax
import jax.numpy as jnp
from jax import lax
from jax.experimental import pallas as pl
from jax.experimental.pallas import tpu as pltpu
from jax.sharding import PartitionSpec as P

SPAN = 128
TILE = 256
RIM = 16
VMEM = 50 * 1024 * 1024
SMALL = 16 * 1024 * 1024
LOG2E = math.log2(math.e)
BF16 = jnp.bfloat16
F32 = jnp.float32


def halves(left, right):
    lane = lax.broadcasted_iota(jnp.int32, left.shape, 1)
    return jnp.where(lane < left.shape[1] // 2, left, right)


def spread(columns, index):
    return jnp.broadcast_to(columns[:, index : index + 1], (columns.shape[0], SPAN))


def convolve(rows_ref, taps_ref, base, left):
    cols = pl.ds(left, SPAN)
    accum = jnp.broadcast_to(taps_ref[4:5, cols], (SPAN, SPAN))
    for tap in range(4):
        accum = accum + taps_ref[tap : tap + 1, cols] * rows_ref[pl.ds(base + RIM - 3 + tap, SPAN), cols]
    half = 0.5 * accum
    return half * jnp.tanh(half) + half


def project(tok_ref, w_ref, rows_ref):
    out = jnp.dot(tok_ref[...], w_ref[...], preferred_element_type=F32)
    rows_ref[...] = out.astype(BF16).astype(F32)


def running_sum(row):
    place = lax.broadcasted_iota(jnp.int32, row.shape, 1)
    by = 1
    while by < row.shape[1]:
        row = row + jnp.where(place >= by, pltpu.roll(row, by, 1), 0.0)
        by *= 2
    return row


def decay_kernel(raw_ref, rate_ref, decay_ref, grow_ref, reach_ref, tails_ref, steps_ref, rows_ref, tail_ref, cols_ref):
    pairs = TILE // SPAN
    heads = 2 * pairs
    tiles = cols_ref.shape[0]
    count = raw_ref.shape[0] // tiles
    blocks = count // heads
    tile = pl.program_id(0)

    @pl.when(tile == 0)
    def _():
        raw = raw_ref[...]
        steps = jnp.maximum(raw, 0.0) + jnp.log1p(jnp.exp(-jnp.abs(raw)))
        rows = running_sum(rate_ref[...] * steps)
        totals = jnp.broadcast_to(rows[:, SPAN - 1 :], rows.shape)
        steps_ref[...] = steps
        rows_ref[...] = rows
        tail_ref[...] = jnp.exp2(jnp.minimum(totals - rows, 0.0)) * steps
        block = lax.rem(lax.broadcasted_iota(jnp.int32, rows.shape, 0), count) // heads
        before = jnp.where(block >= 1, pltpu.roll(totals, heads, 0), 0.0)
        by = 1
        while by < blocks:
            before = before + jnp.where(block >= by, pltpu.roll(before, by * heads, 0), 0.0)
            by *= 2
        full = rows + before
        padding = jnp.zeros((SPAN - 2 * count, SPAN), F32)
        for each in range(tiles):
            mine = slice(each * count, (each + 1) * count)
            cols_ref[each] = jnp.concatenate([rows[mine], full[mine], padding], axis=0).T

    mine = pl.ds(pl.multiple_of(tile * count, 8), count)
    cols = cols_ref[tile]
    rows, steps, tails = rows_ref[mine, :], steps_ref[mine, :], tail_ref[mine, :]
    for block in range(blocks):
        here = pl.ds(block * SPAN, SPAN)
        for pair in range(pairs):
            lanes = pl.ds(pair * SPAN, SPAN)
            first = block * heads + 2 * pair
            cums = [spread(cols, first), spread(cols, first + 1)]
            for head, cum in enumerate(cums):
                at = first + head
                decay = jnp.exp2(jnp.minimum(cum - rows[at : at + 1], 0.0)) * steps[at : at + 1]
                decay_ref[0, pair, here, pl.ds(head * SPAN, SPAN)] = decay.astype(BF16)
                row = block * pairs + pair
                tails_ref[0, row : row + 1, pl.ds(head * SPAN, SPAN)] = tails[at : at + 1]
            grow_ref[0, here, lanes] = jnp.exp2(halves(*cums)).astype(BF16)
            reach = halves(spread(cols, count + first), spread(cols, count + first + 1))
            reach_ref[0, here, lanes] = jnp.exp2(reach).astype(BF16)


def scores_of(taps_ref, c_ref, bt_ref, scores_ref, rows_ref):
    row = lax.broadcasted_iota(jnp.int32, (SPAN, SPAN), 0)
    col = lax.broadcasted_iota(jnp.int32, (SPAN, SPAN), 1)
    for block in range(scores_ref.shape[0]):
        here = pl.ds(block * SPAN, SPAN)
        b_t = convolve(rows_ref, taps_ref, block * SPAN, 0).astype(BF16).astype(F32).T
        c_rows = convolve(rows_ref, taps_ref, block * SPAN, SPAN).astype(BF16)
        bt_ref[:, here] = b_t
        c_ref[here, :] = c_rows
        scores = jnp.dot(c_rows, b_t.astype(BF16), preferred_element_type=F32)
        scores = jnp.where(row >= col, scores, 0.0).astype(BF16)
        scores_ref[block] = jnp.concatenate([scores, scores], axis=1)


def scan_tile(taps_ref, c_ref, bt_ref, scores_ref, decay_ref, grow_ref, tails_ref, lanes_ref, y_ref, state_ref, sent_ref, rows_ref, upper, extra_ref):
    blocks = scores_ref.shape[0]
    pairs = TILE // SPAN
    states = [None] * pairs
    for block in range(blocks):
        here = pl.ds(block * SPAN, SPAN)
        for pair in range(pairs):
            lanes = pl.ds(pair * SPAN, SPAN)
            x = convolve(rows_ref, taps_ref, block * SPAN, pair * SPAN).astype(BF16).astype(F32)
            mix = decay_ref[0, pair, here, :] * scores_ref[block]
            b_t = bt_ref[:, here]
            at = block * pairs + pair
            tail = jnp.concatenate([b_t, b_t], axis=1) * tails_ref[0, at : at + 1, :]
            zero = jnp.zeros_like(x)
            stacked = jnp.concatenate([halves(x, zero), halves(zero, x)], axis=0).astype(BF16)
            weights = jnp.concatenate([mix, tail.astype(BF16)], axis=0)
            out = jnp.dot(weights, stacked, preferred_element_type=F32)
            y, state = out[:SPAN], out[SPAN:]
            if block > 0:
                carried = jnp.dot(c_ref[here, :], states[pair].astype(BF16), preferred_element_type=F32)
                y = y + grow_ref[0, here, lanes].astype(F32) * carried
                state = lanes_ref[0, block : block + 1, lanes] * states[pair] + state
            y_ref[0, here, lanes] = (y + lanes_ref[0, blocks : blocks + 1, lanes] * x).astype(BF16)
            states[pair] = state
    for pair in range(pairs):
        lanes = pl.ds(pair * SPAN, SPAN)
        if upper is None:
            state_ref[:, lanes] = states[pair]
            sent_ref[:, lanes] = states[pair].astype(BF16)
            continue
        half = SPAN // 2
        low, high = states[pair][:half], states[pair][half:]
        state_ref[:, lanes] = jnp.where(upper, high, low)
        sent_ref[:half, lanes] = jnp.where(upper, low, high).astype(BF16)
    if extra_ref is not None:
        sent_ref[SPAN // 2 :, :] = extra_ref[...]


def scan_kernel(leads, extras, tiles, piece_count, lead_at, base, *refs):
    offsets, place = refs[:2]
    refs = refs[1:]
    pieces = refs[1 : 1 + piece_count]
    rim_ref, tokens_ref, taps_ref, decay_ref, grow_ref, tails_ref, lanes_ref, taps_bc_ref = refs[1 + piece_count : 9 + piece_count]
    rest = refs[9 + piece_count : -6]
    tok_ref, w_a, w_b, rows_a, rows_b, sems = refs[-6:]
    extra_ref = None
    if extras:
        extra_ref, *rest = rest
    if leads:
        y_ref, state_ref, sent_ref, c_ref, bt_ref, scores_ref = rest
    else:
        c_ref, bt_ref, scores_ref, y_ref, state_ref, sent_ref = rest
    step = pl.program_id(0)
    items = tiles + leads
    w_refs, rows_refs = (w_a, w_b), (rows_a, rows_b)

    def fetch(item, slot):
        tile = item - leads + base
        if leads:
            tile = jnp.where(item == 0, lead_at, tile)
        index = 0
        for piece in pieces:
            rows = piece.shape[2]
            for part in range(piece.shape[0]):
                target = pl.multiple_of(offsets[index], 16)
                pltpu.make_async_copy(
                    piece.at[part, tile], w_refs[slot].at[pl.ds(target, rows)], sems.at[slot]
                ).start()
                index += 1

    def arrive(slot):
        pltpu.make_async_copy(w_refs[slot], w_refs[slot], sems.at[slot]).wait()

    def multiply(slot):
        project(tok_ref, w_refs[slot], rows_refs[slot])

    def finish(slot):
        scan_tile(
            taps_ref, c_ref, bt_ref, scores_ref, decay_ref, grow_ref, tails_ref, lanes_ref, y_ref, state_ref, sent_ref, rows_refs[slot],
            place[0] == 1 if state_ref.shape[0] < SPAN else None,
            extra_ref,
        )

    def lead(slot):
        scores_of(taps_bc_ref, c_ref, bt_ref, scores_ref, rows_refs[slot])

    @pl.when(step == 0)
    def _():
        copies = [
            pltpu.make_async_copy(rim_ref, tok_ref.at[pl.ds(0, RIM)], sems.at[2]),
            pltpu.make_async_copy(tokens_ref, tok_ref.at[pl.ds(RIM, tokens_ref.shape[0])], sems.at[3]),
        ]
        for copy in copies:
            copy.start()
        fetch(0, 0)
        for copy in copies:
            copy.wait()
        arrive(0)
        if items > 1:
            fetch(1, 1)
        multiply(0)

    if leads and items > 1:

        @pl.when(step == 1)
        def _():
            arrive(1)
            if items > 2:
                fetch(2, 0)
            multiply(1)
            lead(0)

    for slot in (0, 1):
        low = 1 + leads

        @pl.when((step >= low) & (step < items) & (lax.rem(step, 2) == slot))
        def _():
            arrive(slot)

            @pl.when(step + 1 < items)
            def _():
                fetch(step + 1, 1 - slot)

            multiply(slot)
            finish(1 - slot)

    @pl.when(step == items)
    def _():
        finish((items - 1) % 2)


def norm_kernel(count, place_ref, y_ref, c_ref, reach_ref, gain_ref, gather_ref, *rest):
    out_ref = rest[-1]
    state = rest[0][...]
    if count == 2:
        ours, theirs = state, rest[1][...]
        upper = place_ref[0] == 1
        low, high = jnp.where(upper, theirs, ours), jnp.where(upper, ours, theirs)
        state = jnp.concatenate([low, high], axis=0)
    carried = jnp.dot(c_ref[...], state, preferred_element_type=F32)
    ssd = y_ref[0].astype(F32) + reach_ref[0].astype(F32) * carried
    square = jnp.minimum(ssd * ssd, 1e38).astype(BF16)
    mean = jnp.dot(square, gather_ref[...], preferred_element_type=F32)
    out_ref[...] = (ssd * lax.rsqrt(mean + 1e-05) * gain_ref[...]).astype(BF16)


def whole(shape):
    return pl.BlockSpec(shape, lambda *_: (0,) * len(shape))


def params(limit=VMEM):
    return pltpu.CompilerParams(vmem_limit_bytes=limit)


def run_decay(raw, rate):
    tiles, count = raw.shape[:2]
    pairs = TILE // SPAN
    table = pltpu.VMEM((tiles * count, SPAN), F32)
    tok_count = count // (2 * pairs) * SPAN
    rounds = pairs * tok_count // SPAN
    tail_rows = rounds + -rounds % 8
    return pl.pallas_call(
        decay_kernel,
        grid=(tiles,),
        in_specs=[
            whole((tiles * count, SPAN)),
            whole((tiles * count, 1)),
        ],
        out_specs=[
            pl.BlockSpec((1, pairs, tok_count, 2 * SPAN), lambda i: (i, 0, 0, 0)),
            pl.BlockSpec((1, tok_count, TILE), lambda i: (i, 0, 0)),
            pl.BlockSpec((1, tok_count, TILE), lambda i: (i, 0, 0)),
            pl.BlockSpec((1, tail_rows, 2 * SPAN), lambda i: (i, 0, 0)),
        ],
        out_shape=[
            jax.ShapeDtypeStruct((tiles, pairs, tok_count, 2 * SPAN), BF16),
            jax.ShapeDtypeStruct((tiles, tok_count, TILE), BF16),
            jax.ShapeDtypeStruct((tiles, tok_count, TILE), BF16),
            jax.ShapeDtypeStruct((tiles, tail_rows, 2 * SPAN), F32),
        ],
        scratch_shapes=[table, table, table, pltpu.VMEM((tiles, SPAN, SPAN), F32)],
        compiler_params=params(),
        cost_estimate=pl.CostEstimate(flops=10_000_000_000, bytes_accessed=16_000_000, transcendentals=0),
        name="decays",
    )(raw.reshape(tiles * count, SPAN), rate.reshape(tiles * count, 1))


def run_scan(pieces, offsets, place, lead_at, base, rim, tokens, taps, shared, decay, grow, tails, lanes, first, tiles, extra=None):
    tok_count, depth = tokens.shape
    rows = tok_count + RIM
    blocks = tok_count // SPAN
    leads = 1 if shared is None else 0
    behind = lambda i: jnp.clip(i - 1 - leads, 0, tiles - 1)
    per_tile = lambda array: pl.BlockSpec((1,) + array.shape[1:], lambda i: (behind(i) + first, 0, 0))
    held = SPAN // 2 if place is not None else SPAN
    place = jnp.zeros((1,), jnp.int32) if place is None else place
    ins = [offsets, place, *pieces, rim, tokens, taps, decay, grow, tails, lanes, taps]
    specs = [pl.BlockSpec(memory_space=pltpu.SMEM)] * 2
    specs += [pl.BlockSpec(memory_space=pl.ANY)] * (len(pieces) + 2)
    specs += [
        pl.BlockSpec((8, TILE), lambda i: (0, behind(i) + first)),
        pl.BlockSpec((1,) + decay.shape[1:], lambda i: (behind(i) + first, 0, 0, 0)),
        per_tile(grow),
        per_tile(tails),
        per_tile(lanes),
        pl.BlockSpec((8, TILE), lambda i: (0, taps.shape[1] // TILE - 1)),
    ]
    out_shape = [
        jax.ShapeDtypeStruct((tiles, tok_count, TILE), BF16),
        jax.ShapeDtypeStruct((held, tiles * TILE), F32),
        jax.ShapeDtypeStruct((held + (0 if extra is None else extra.shape[0]), tiles * TILE), BF16),
    ]
    out_specs = [
        pl.BlockSpec((1, tok_count, TILE), lambda i: (behind(i), 0, 0)),
        pl.BlockSpec((held, TILE), lambda i: (0, behind(i))),
        pl.BlockSpec((out_shape[2].shape[0], TILE), lambda i: (0, behind(i))),
    ]
    shared_shape = [
        jax.ShapeDtypeStruct((tok_count, SPAN), BF16),
        jax.ShapeDtypeStruct((SPAN, tok_count), F32),
        jax.ShapeDtypeStruct((blocks, SPAN, 2 * SPAN), BF16),
    ]
    shared_specs = [whole(each.shape) for each in shared_shape]
    extras = 0 if extra is None else extra.shape[0]
    if extras:
        ins.append(extra)
        specs.append(pl.BlockSpec((extras, TILE), lambda i: (0, behind(i))))
    if leads:
        out_shape += shared_shape
        out_specs += shared_specs
    else:
        ins += shared
        specs += shared_specs
    outs = pl.pallas_call(
        lambda *refs: scan_kernel(leads, extras, tiles, len(pieces), lead_at, base, *refs),
        grid=(tiles + leads + 1,),
        in_specs=specs,
        out_specs=out_specs,
        out_shape=out_shape,
        scratch_shapes=[pltpu.VMEM((rows, depth), BF16)]
        + [pltpu.VMEM((depth, TILE), BF16)] * 2
        + [pltpu.VMEM((rows, TILE), F32)] * 2
        + [pltpu.SemaphoreType.DMA((4,))],
        compiler_params=params(),
        cost_estimate=pl.CostEstimate(flops=3_000_000_000 * tiles, bytes_accessed=3_000_000 * tiles, transcendentals=0),
        name="project_scan",
    )(*ins)
    return *outs[:3], (list(outs[3:]) if leads else shared)


def run_norm(out, place, y, c_rows, reach, gain, gather, state, first, base, tiles, width):
    tok_count = c_rows.shape[0]
    ins = [place, y, c_rows, reach, gain, gather, *state]
    specs = [
        pl.BlockSpec(memory_space=pltpu.SMEM),
        pl.BlockSpec((1, tok_count, TILE), lambda i: (i + base, 0, 0)),
        whole(c_rows.shape),
        pl.BlockSpec((1, tok_count, TILE), lambda i: (i + first, 0, 0)),
        pl.BlockSpec((1, TILE), lambda i: (0, i + first)),
        whole(gather.shape),
    ]
    specs += [pl.BlockSpec((part.shape[0], TILE), lambda i: (0, i + base)) for part in state]
    aliases = {}
    if out is not None:
        aliases = {len(ins): 0}
        ins.append(out)
        specs.append(pl.BlockSpec(memory_space=pl.ANY))
    return pl.pallas_call(
        lambda *refs: norm_kernel(len(state), *refs),
        grid=(tiles,),
        in_specs=specs,
        out_specs=pl.BlockSpec((tok_count, TILE), lambda i: (0, i + first)),
        out_shape=jax.ShapeDtypeStruct((tok_count, width), BF16),
        input_output_aliases=aliases,
        compiler_params=params(SMALL),
        cost_estimate=pl.CostEstimate(flops=400_000_000 * tiles, bytes_accessed=5 * tok_count * TILE * tiles, transcendentals=0),
        name="head_norm",
    )(*ins)


def shifted(value, z_by, y_by, z_count, y_count):
    pairs = []
    for z in range(z_count - z_by):
        for y in range(y_count):
            pairs.append((z * y_count + y, (z + z_by) * y_count + (y + y_by) % y_count))
    return lax.ppermute(value, "seq", pairs)


def stack(*arrays):
    return jnp.concatenate(arrays, axis=0)


def together(*arrays):
    return lax.optimization_barrier(arrays)


class Links:
    def __init__(self, z_count, y_count):
        self.z_count, self.y_count = z_count, y_count

    def index(self, x, core, z, y):
        return (x * 2 + core) * self.z_count * self.y_count + z * self.y_count + y

    def send(self, value, target):
        pairs = []
        for x in range(2):
            for core in range(2):
                for z in range(self.z_count):
                    for y in range(self.y_count):
                        pairs.append((self.index(x, core, z, y), self.index(*target(x, core, z, y))))
        return lax.ppermute(value, ("dp", "seq"), pairs)

    def along_z(self, value, by):
        return self.send(value, lambda x, core, z, y: (x, core, (z + by) % self.z_count, y))

    def first(self, value):
        return self.send(value, lambda x, core, z, y: (x, core, z, 1 - y) if core else (1 - x, core, z, y))

    def second(self, value):
        return self.send(value, lambda x, core, z, y: (1 - x, core, z, y) if core else (x, core, z, 1 - y))

    def sibling(self, value):
        return self.send(value, lambda x, core, z, y: (x, 1 - core, z, y))

    def gather(self, own, early, decays):
        z1, z3, own_1, own_2, own = together(
            self.along_z(own, 1), self.along_z(own, 3), self.first(own), self.second(own), own
        )
        near = stack(z1, z3)
        z2, near_1, near_2, own_12, *early = together(
            self.along_z(own, 2), self.first(near), self.second(near), self.second(own_1), *early
        )
        mine = stack(own, own_1, own_2, own_12)
        far_1, far_2, near_12, mine_other, *decays = together(
            self.first(z2), self.second(z2), self.second(near_1), self.sibling(mine), *decays(early)
        )
        beside = stack(near, near_1, near_2, near_12)
        far = stack(z2, far_1, far_2)
        far_12, beside_other, far_other = together(self.second(far_1), self.sibling(beside), self.sibling(far))
        return [mine, beside, far, far_12, mine_other, beside_other, far_other, self.sibling(far_12)], early, decays

    def owners(self):
        dp, seq = lax.axis_index("dp"), lax.axis_index("seq")
        x, core = dp // 2, dp % 2
        z, y = seq // self.y_count, seq % self.y_count
        places = []
        for at in (core, 1 - core):
            for hops in ((0,), (1, 3), (2,)):
                for by_first, by_second in ((0, 0), (1, 0), (0, 1), (1, 1)):
                    for hop in hops:
                        turn_x = jnp.where(at == 0, by_first, by_second)
                        turn_y = jnp.where(at == 0, by_second, by_first)
                        other = (z - hop + self.z_count) % self.z_count
                        places.append(self.index((x + turn_x) % 2, at, other, (y + turn_y) % 2))
        return jnp.stack(places).astype(jnp.int32)


def expand(per_head, head_size):
    return jnp.repeat(per_head, head_size, axis=-1)


def local(tokens, w_xbc, conv_weight, conv_bias, a_log, dt_in, d_skip, norm_gain):
    token_rows = tokens[0]
    tok_count = token_rows.shape[0]
    heads = a_log.shape[0]
    width_x = norm_gain.shape[0]
    head_size = width_x // heads
    channels = w_xbc.shape[1]
    blocks = tok_count // SPAN
    tiles = width_x // TILE
    per_tile = TILE // head_size
    seq_count = lax.axis_size("seq")
    z_count = 4
    y_count = seq_count // z_count
    y_mine = lax.rem(lax.axis_index("seq"), y_count)

    after = lambda rows: lax.ppermute(rows, "seq", [(i, i + 1) for i in range(seq_count - 1)])
    rim_rows = token_rows[tok_count - RIM :]
    taps = jnp.concatenate([conv_weight, conv_bias[None], jnp.zeros((3, channels), F32)], axis=0)
    rate = -LOG2E * jnp.exp(a_log)
    totals = rate[:, None] * jnp.sum(jax.nn.softplus(dt_in[0]).reshape(heads, blocks, SPAN), axis=2)
    head_of = jnp.arange(TILE) // head_size
    gather = jnp.where(head_of[:, None] == head_of[None, :], 1.0 / head_size, 0.0).astype(BF16)

    def lane_rows(totals):
        rows = jnp.concatenate([jnp.exp2(totals).T, d_skip[None]], axis=0)
        rows = jnp.pad(expand(rows, head_size), ((0, -(blocks + 1) % 8), (0, 0)))
        return rows.reshape(rows.shape[0], tiles, TILE).transpose(1, 0, 2)

    def along_y(totals):
        own = jnp.sum(totals, axis=1)
        side = jnp.broadcast_to(jnp.pad(own, (0, SPAN - heads))[None], (8, SPAN))
        return [own] + [shifted(side, 0, k, z_count, y_count)[0, :heads] for k in range(1, y_count)]

    def along_z(y_decay):
        own = jnp.broadcast_to(jnp.pad(sum(y_decay), (0, SPAN - heads))[None], (8, SPAN))
        return [shifted(own, k, 0, z_count, y_count)[0, :heads] for k in range(1, z_count - 1)]

    def z_weights(z_decay):
        reach = [jnp.zeros((heads,), F32)]
        for decay in z_decay:
            reach.append(reach[-1] + decay)
        return reach[1:]

    by_block = lambda rows: rows.reshape(tiles, per_tile, blocks, -1).swapaxes(1, 2).reshape(tiles, blocks * per_tile, -1)
    raw = by_block(dt_in[0])
    rates = by_block(jnp.broadcast_to(rate[:, None], (heads, blocks)))
    lanes = lane_rows(totals)
    if lax.axis_size("dp") == 4 and seq_count == 8:
        split = tiles // 2
        links = Links(z_count, y_count)
        row_count = w_xbc.shape[0]
        by_column = w_xbc.reshape(row_count, channels // TILE, TILE).swapaxes(0, 1)[None]
        late_w = lax.all_gather(by_column[:, :split], ("dp", "seq"), axis=0, tiled=True)
        late_rows = jnp.arange(lax.axis_size("dp") * seq_count, dtype=jnp.int32) * row_count
        early_rows = links.owners() * row_count

        kept = expand(jnp.exp2(jnp.sum(totals, axis=1)), head_size)
        wide = (tiles - split) * TILE
        rest = jnp.pad(kept[: split * TILE], (0, -(split * TILE) % wide)).reshape(-1, wide)
        own_kept = jnp.concatenate([kept[None, split * TILE :], rest], axis=0)
        extra = jnp.pad(own_kept, ((0, 16 - own_kept.shape[0]), (0, 0))).astype(BF16)

        early_w, prepared, (decay, grow, reach, tails) = links.gather(
            by_column[:, split:],
            (taps, lanes, gather, early_rows, late_rows, after(rim_rows), own_kept, extra, raw, rates),
            lambda ready: run_decay(*ready[8:]),
        )
        taps, lanes, gather, early_rows, late_rows, rim, own_kept, extra = prepared[:8]
        calls = [(early_w, early_rows, split, 0, tiles - split), ([late_w], late_rows, 0, 0, split)]
        lead_at = tiles - split
        halved = y_mine.astype(jnp.int32)[None]

        upper = y_mine == 1
        swap = lambda value: shifted(value, 0, 1, z_count, y_count)

        half = SPAN // 2

        def plane_of(own, other, upper_kept, rows=None):
            other = other[:half].astype(F32)
            plane = jnp.where(upper, own + upper_kept * other, upper_kept * own + other)
            if rows is not None:
                plane = jnp.concatenate([plane, jnp.pad(rows, ((0, 16 - rows.shape[0]), (0, 0)))], axis=0)
            plane = plane.astype(BF16)
            return [shifted(plane, k, 0, z_count, y_count) for k in range(1, z_count)]

        def halves_of(own, other, below, lower_kept, z_kept):
            base = below[0][:half].astype(F32)
            through = 1.0
            for kept, part in zip(z_kept, below[1:]):
                through = through * kept
                base = base + through * part[:half].astype(F32)
            above = lower_kept * base + jnp.where(upper, other[:half].astype(F32), own)
            theirs = swap(jnp.where(upper, base, above).astype(BF16))
            return [jnp.where(upper, above, base).astype(BF16), theirs]

    else:
        full = lax.all_gather(w_xbc, ("dp", "seq"), axis=0, tiled=True)
        full = full.reshape(full.shape[0], channels // TILE, TILE).swapaxes(0, 1)[None]
        first_row = jnp.zeros((1,), jnp.int32)
        calls = [([full], first_row, first, first, min(5, tiles - first)) for first in range(0, tiles, 5)]
        lead_at = tiles
        rim = after(rim_rows)
        halved = None
        decay, grow, reach, tails = run_decay(raw, rates)
        y_decay = along_y(totals)
        z_reach = z_weights(along_z(y_decay))

        def beside(sent):
            return [shifted(sent, 0, k, z_count, y_count) for k in range(1, y_count)]

        def incoming(own, parts, lane):
            place = [lax.rem(y_mine - k + y_count, y_count) for k in range(y_count)]
            spread_lanes = lambda row: expand(row, head_size)[lane]
            inner = lambda keep: sum(jnp.where(keep(m), y_decay[m], 0.0) for m in range(y_count))
            parts = [own] + [part.astype(F32) for part in parts]
            plane, above = 0.0, 0.0
            for k, part in enumerate(parts):
                after = inner(lambda m: place[m] > place[k])
                until = inner(lambda m: (place[m] > place[k]) & (place[m] < y_mine))
                plane = plane + spread_lanes(jnp.exp2(after)) * part
                above = above + spread_lanes(jnp.where(place[k] < y_mine, jnp.exp2(until), 0.0)) * part
            inside = inner(lambda m: place[m] < y_mine)
            plane = plane.astype(BF16)
            for k in range(1, z_count):
                along = inside if k == 1 else inside + z_reach[k - 2]
                above = above + spread_lanes(jnp.exp2(along)) * shifted(plane, k, 0, z_count, y_count).astype(F32)
            return [above.astype(BF16)]

    def scan(call, shared, extra=None):
        pieces, places, first, base, count = call
        return run_scan(
            pieces, places, halved, lead_at, base, rim, token_rows, taps, shared, decay, grow, tails, lanes, first, count, extra
        )

    def norm(out, y, state, first, base, count):
        place = y_mine.astype(jnp.int32)[None]
        return run_norm(
            out, place, y, shared[0], reach, norm_gain[None], gather, state, first + base, base, count, width_x
        )

    if halved is None:
        shared, out = None, None
        pending = []
        for call in calls:
            y, own, sent, shared = scan(call, shared)
            first, count = call[2], call[4]
            pending.append((y, incoming(own, beside(sent), slice(first * TILE, (first + count) * TILE)), first, 0, count))
        for each in pending:
            out = norm(out, *each)
        return out[None]

    (_, _, first_a, _, count_a), (_, _, first_b, _, count_b) = calls
    y_a, own_a, sent_a, shared = scan(calls[0], None, extra)
    other_a = swap(sent_a)
    kept_rows = slice(half, half + own_kept.shape[0])
    later = lambda rows: rows[1:].reshape(-1)[: count_b * TILE]
    other_kept = other_a[kept_rows].astype(F32)
    lower_kept = jnp.where(upper, other_kept, own_kept)
    upper_kept = jnp.where(upper, own_kept, other_kept)
    pieces, other_a = together(calls[1][0], other_a)
    below_a = plane_of(own_a, other_a, upper_kept[0], lower_kept * upper_kept)
    y_b, own_b, sent_b, _ = scan((pieces, *calls[1][1:]), shared)
    sent_b, *below_a = together(sent_b, *below_a)
    other_b = swap(sent_b)
    z_kept = [part[kept_rows].astype(F32) for part in below_a]
    state_a = halves_of(own_a, other_a, below_a, lower_kept[0], [kept[0] for kept in z_kept])
    below_b = plane_of(own_b, other_b, later(upper_kept))
    out = norm(None, y_a, state_a, first_a, 0, count_a // 2)
    out = norm(out, y_a, state_a, first_a, count_a // 2, count_a - count_a // 2)
    out, *below_b = together(out, *below_b)
    state_b = halves_of(own_b, other_b, below_b, later(lower_kept), [later(kept) for kept in z_kept])
    out = norm(out, y_b, state_b, first_b, 0, count_b)
    return out[None]


def solution(mesh):
    return jax.shard_map(
        local,
        mesh=mesh,
        in_specs=(
            P("dp", "seq", None),
            P(("dp", "seq"), None),
            P(),
            P(),
            P(),
            P("dp", None, "seq"),
            P(),
            P(),
        ),
        out_specs=P("dp", "seq", None),
        check_vma=False,
    )
```

```python
import math

import jax
import jax.numpy as jnp
from jax import lax
from jax.experimental import pallas as pl
from jax.experimental.pallas import tpu as pltpu
from jax.sharding import PartitionSpec as P

SPAN = 128
TILE = 256
RIM = 16
VMEM = 48 * 1024 * 1024
SMALL = 16 * 1024 * 1024
LOG2E = math.log2(math.e)
BF16 = jnp.bfloat16
F32 = jnp.float32


def halves(left, right):
    lane = lax.broadcasted_iota(jnp.int32, left.shape, 1)
    return jnp.where(lane < left.shape[1] // 2, left, right)


def spread(columns, index):
    return jnp.broadcast_to(columns[:, index : index + 1], (columns.shape[0], SPAN))


def convolve(rows_ref, taps_ref, base, left):
    cols = pl.ds(left, SPAN)
    accum = jnp.broadcast_to(taps_ref[4:5, cols], (SPAN, SPAN))
    for tap in range(4):
        accum = accum + taps_ref[tap : tap + 1, cols] * rows_ref[pl.ds(base + RIM - 3 + tap, SPAN), cols]
    half = 0.5 * accum
    return half * jnp.tanh(half) + half


def project(tok_ref, w_ref, rows_ref):
    out = jnp.dot(tok_ref[...], w_ref[...], preferred_element_type=F32)
    rows_ref[...] = out.astype(BF16).astype(F32)


def running_sum(row):
    place = lax.broadcasted_iota(jnp.int32, row.shape, 1)
    by = 1
    while by < row.shape[1]:
        row = row + jnp.where(place >= by, pltpu.roll(row, by, 1), 0.0)
        by *= 2
    return row


def decay_kernel(raw_ref, rate_ref, decay_ref, grow_ref, reach_ref, tails_ref, steps_ref, rows_ref, tail_ref, cols_ref):
    pairs = TILE // SPAN
    heads = 2 * pairs
    tiles = cols_ref.shape[0]
    count = raw_ref.shape[0] // tiles
    blocks = count // heads
    tile = pl.program_id(0)

    @pl.when(tile == 0)
    def _():
        raw = raw_ref[...]
        steps = jnp.maximum(raw, 0.0) + jnp.log1p(jnp.exp(-jnp.abs(raw)))
        rows = running_sum(rate_ref[...] * steps)
        totals = jnp.broadcast_to(rows[:, SPAN - 1 :], rows.shape)
        steps_ref[...] = steps
        rows_ref[...] = rows
        tail_ref[...] = jnp.exp2(jnp.minimum(totals - rows, 0.0)) * steps
        block = lax.rem(lax.broadcasted_iota(jnp.int32, rows.shape, 0), count) // heads
        before = jnp.where(block >= 1, pltpu.roll(totals, heads, 0), 0.0)
        by = 1
        while by < blocks:
            before = before + jnp.where(block >= by, pltpu.roll(before, by * heads, 0), 0.0)
            by *= 2
        full = rows + before
        padding = jnp.zeros((SPAN - 2 * count, SPAN), F32)
        for each in range(tiles):
            mine = slice(each * count, (each + 1) * count)
            cols_ref[each] = jnp.concatenate([rows[mine], full[mine], padding], axis=0).T

    mine = pl.ds(pl.multiple_of(tile * count, 8), count)
    cols = cols_ref[tile]
    rows, steps, tails = rows_ref[mine, :], steps_ref[mine, :], tail_ref[mine, :]
    for block in range(blocks):
        here = pl.ds(block * SPAN, SPAN)
        for pair in range(pairs):
            lanes = pl.ds(pair * SPAN, SPAN)
            first = block * heads + 2 * pair
            cums = [spread(cols, first), spread(cols, first + 1)]
            for head, cum in enumerate(cums):
                at = first + head
                decay = jnp.exp2(jnp.minimum(cum - rows[at : at + 1], 0.0)) * steps[at : at + 1]
                decay_ref[0, pair, here, pl.ds(head * SPAN, SPAN)] = decay.astype(BF16)
                row = block * pairs + pair
                tails_ref[0, row : row + 1, pl.ds(head * SPAN, SPAN)] = tails[at : at + 1]
            grow_ref[0, here, lanes] = jnp.exp2(halves(*cums)).astype(BF16)
            reach = halves(spread(cols, count + first), spread(cols, count + first + 1))
            reach_ref[0, here, lanes] = jnp.exp2(reach).astype(BF16)


def scores_of(taps_ref, c_ref, bt_ref, scores_ref, rows_ref):
    row = lax.broadcasted_iota(jnp.int32, (SPAN, SPAN), 0)
    col = lax.broadcasted_iota(jnp.int32, (SPAN, SPAN), 1)
    for block in range(scores_ref.shape[0]):
        here = pl.ds(block * SPAN, SPAN)
        b_t = convolve(rows_ref, taps_ref, block * SPAN, 0).astype(BF16).astype(F32).T
        c_rows = convolve(rows_ref, taps_ref, block * SPAN, SPAN).astype(BF16)
        bt_ref[:, here] = b_t
        c_ref[here, :] = c_rows
        scores = jnp.dot(c_rows, b_t.astype(BF16), preferred_element_type=F32)
        scores = jnp.where(row >= col, scores, 0.0).astype(BF16)
        scores_ref[block] = jnp.concatenate([scores, scores], axis=1)


def scan_tile(taps_ref, c_ref, bt_ref, scores_ref, decay_ref, grow_ref, tails_ref, lanes_ref, y_ref, state_ref, sent_ref, rows_ref, upper, extra_ref):
    blocks = scores_ref.shape[0]
    pairs = TILE // SPAN
    states = [None] * pairs
    for block in range(blocks):
        here = pl.ds(block * SPAN, SPAN)
        for pair in range(pairs):
            lanes = pl.ds(pair * SPAN, SPAN)
            x = convolve(rows_ref, taps_ref, block * SPAN, pair * SPAN).astype(BF16).astype(F32)
            mix = decay_ref[0, pair, here, :] * scores_ref[block]
            b_t = bt_ref[:, here]
            at = block * pairs + pair
            tail = jnp.concatenate([b_t, b_t], axis=1) * tails_ref[0, at : at + 1, :]
            zero = jnp.zeros_like(x)
            stacked = jnp.concatenate([halves(x, zero), halves(zero, x)], axis=0).astype(BF16)
            weights = jnp.concatenate([mix, tail.astype(BF16)], axis=0)
            out = jnp.dot(weights, stacked, preferred_element_type=F32)
            y, state = out[:SPAN], out[SPAN:]
            if block > 0:
                carried = jnp.dot(c_ref[here, :], states[pair].astype(BF16), preferred_element_type=F32)
                y = y + grow_ref[0, here, lanes].astype(F32) * carried
                state = lanes_ref[0, block : block + 1, lanes] * states[pair] + state
            y_ref[0, here, lanes] = (y + lanes_ref[0, blocks : blocks + 1, lanes] * x).astype(BF16)
            states[pair] = state
    for pair in range(pairs):
        lanes = pl.ds(pair * SPAN, SPAN)
        if upper is None:
            state_ref[:, lanes] = states[pair]
            sent_ref[:, lanes] = states[pair].astype(BF16)
            continue
        half = SPAN // 2
        low, high = states[pair][:half], states[pair][half:]
        state_ref[:, lanes] = jnp.where(upper, high, low)
        sent_ref[:half, lanes] = jnp.where(upper, low, high).astype(BF16)
    if extra_ref is not None:
        sent_ref[SPAN // 2 :, :] = extra_ref[...]


def scan_kernel(leads, extras, tiles, piece_count, lead_at, base, *refs):
    offsets, place = refs[:2]
    refs = refs[1:]
    pieces = refs[1 : 1 + piece_count]
    rim_ref, tokens_ref, taps_ref, decay_ref, grow_ref, tails_ref, lanes_ref, taps_bc_ref = refs[1 + piece_count : 9 + piece_count]
    rest = refs[9 + piece_count : -6]
    tok_ref, w_a, w_b, rows_a, rows_b, sems = refs[-6:]
    extra_ref = None
    if extras:
        extra_ref, *rest = rest
    if leads:
        y_ref, state_ref, sent_ref, c_ref, bt_ref, scores_ref = rest
    else:
        c_ref, bt_ref, scores_ref, y_ref, state_ref, sent_ref = rest
    step = pl.program_id(0)
    items = tiles + leads
    w_refs, rows_refs = (w_a, w_b), (rows_a, rows_b)

    def fetch(item, slot):
        tile = item - leads + base
        if leads:
            tile = jnp.where(item == 0, lead_at, tile)
        index = 0
        for piece in pieces:
            rows = piece.shape[2]
            for part in range(piece.shape[0]):
                target = pl.multiple_of(offsets[index], 16)
                pltpu.make_async_copy(
                    piece.at[part, tile], w_refs[slot].at[pl.ds(target, rows)], sems.at[slot]
                ).start()
                index += 1

    def arrive(slot):
        pltpu.make_async_copy(w_refs[slot], w_refs[slot], sems.at[slot]).wait()

    def multiply(slot):
        project(tok_ref, w_refs[slot], rows_refs[slot])

    def finish(slot):
        scan_tile(
            taps_ref, c_ref, bt_ref, scores_ref, decay_ref, grow_ref, tails_ref, lanes_ref, y_ref, state_ref, sent_ref, rows_refs[slot],
            place[0] == 1 if state_ref.shape[0] < SPAN else None,
            extra_ref,
        )

    def lead(slot):
        scores_of(taps_bc_ref, c_ref, bt_ref, scores_ref, rows_refs[slot])

    @pl.when(step == 0)
    def _():
        copies = [
            pltpu.make_async_copy(rim_ref, tok_ref.at[pl.ds(0, RIM)], sems.at[2]),
            pltpu.make_async_copy(tokens_ref, tok_ref.at[pl.ds(RIM, tokens_ref.shape[0])], sems.at[3]),
        ]
        for copy in copies:
            copy.start()
        fetch(0, 0)
        for copy in copies:
            copy.wait()
        arrive(0)
        if items > 1:
            fetch(1, 1)
        multiply(0)

    if leads and items > 1:

        @pl.when(step == 1)
        def _():
            arrive(1)
            if items > 2:
                fetch(2, 0)
            multiply(1)
            lead(0)

    for slot in (0, 1):
        low = 1 + leads

        @pl.when((step >= low) & (step < items) & (lax.rem(step, 2) == slot))
        def _():
            arrive(slot)

            @pl.when(step + 1 < items)
            def _():
                fetch(step + 1, 1 - slot)

            multiply(slot)
            finish(1 - slot)

    @pl.when(step == items)
    def _():
        finish((items - 1) % 2)


def norm_kernel(count, place_ref, y_ref, c_ref, reach_ref, gain_ref, gather_ref, *rest):
    out_ref = rest[-1]
    state = rest[0][...]
    if count == 2:
        ours, theirs = state, rest[1][...]
        upper = place_ref[0] == 1
        low, high = jnp.where(upper, theirs, ours), jnp.where(upper, ours, theirs)
        state = jnp.concatenate([low, high], axis=0)
    carried = jnp.dot(c_ref[...], state, preferred_element_type=F32)
    ssd = y_ref[0].astype(F32) + reach_ref[0].astype(F32) * carried
    square = jnp.minimum(ssd * ssd, 1e38).astype(BF16)
    mean = jnp.dot(square, gather_ref[...], preferred_element_type=F32)
    out_ref[...] = (ssd * lax.rsqrt(mean + 1e-05) * gain_ref[...]).astype(BF16)


def whole(shape):
    return pl.BlockSpec(shape, lambda *_: (0,) * len(shape))


def params(limit=VMEM):
    return pltpu.CompilerParams(vmem_limit_bytes=limit)


def run_decay(raw, rate):
    tiles, count = raw.shape[:2]
    pairs = TILE // SPAN
    table = pltpu.VMEM((tiles * count, SPAN), F32)
    tok_count = count // (2 * pairs) * SPAN
    rounds = pairs * tok_count // SPAN
    tail_rows = rounds + -rounds % 8
    return pl.pallas_call(
        decay_kernel,
        grid=(tiles,),
        in_specs=[
            whole((tiles * count, SPAN)),
            whole((tiles * count, 1)),
        ],
        out_specs=[
            pl.BlockSpec((1, pairs, tok_count, 2 * SPAN), lambda i: (i, 0, 0, 0)),
            pl.BlockSpec((1, tok_count, TILE), lambda i: (i, 0, 0)),
            pl.BlockSpec((1, tok_count, TILE), lambda i: (i, 0, 0)),
            pl.BlockSpec((1, tail_rows, 2 * SPAN), lambda i: (i, 0, 0)),
        ],
        out_shape=[
            jax.ShapeDtypeStruct((tiles, pairs, tok_count, 2 * SPAN), BF16),
            jax.ShapeDtypeStruct((tiles, tok_count, TILE), BF16),
            jax.ShapeDtypeStruct((tiles, tok_count, TILE), BF16),
            jax.ShapeDtypeStruct((tiles, tail_rows, 2 * SPAN), F32),
        ],
        scratch_shapes=[table, table, table, pltpu.VMEM((tiles, SPAN, SPAN), F32)],
        compiler_params=params(),
        cost_estimate=pl.CostEstimate(flops=10_000_000_000, bytes_accessed=16_000_000, transcendentals=0),
        name="decays",
    )(raw.reshape(tiles * count, SPAN), rate.reshape(tiles * count, 1))


def run_scan(pieces, offsets, place, lead_at, base, rim, tokens, taps, shared, decay, grow, tails, lanes, first, tiles, extra=None):
    tok_count, depth = tokens.shape
    rows = tok_count + RIM
    blocks = tok_count // SPAN
    leads = 1 if shared is None else 0
    behind = lambda i: jnp.clip(i - 1 - leads, 0, tiles - 1)
    per_tile = lambda array: pl.BlockSpec((1,) + array.shape[1:], lambda i: (behind(i) + first, 0, 0))
    held = SPAN // 2 if place is not None else SPAN
    place = jnp.zeros((1,), jnp.int32) if place is None else place
    ins = [offsets, place, *pieces, rim, tokens, taps, decay, grow, tails, lanes, taps]
    specs = [pl.BlockSpec(memory_space=pltpu.SMEM)] * 2
    specs += [pl.BlockSpec(memory_space=pl.ANY)] * (len(pieces) + 2)
    specs += [
        pl.BlockSpec((8, TILE), lambda i: (0, behind(i) + first)),
        pl.BlockSpec((1,) + decay.shape[1:], lambda i: (behind(i) + first, 0, 0, 0)),
        per_tile(grow),
        per_tile(tails),
        per_tile(lanes),
        pl.BlockSpec((8, TILE), lambda i: (0, taps.shape[1] // TILE - 1)),
    ]
    out_shape = [
        jax.ShapeDtypeStruct((tiles, tok_count, TILE), BF16),
        jax.ShapeDtypeStruct((held, tiles * TILE), F32),
        jax.ShapeDtypeStruct((held + (0 if extra is None else extra.shape[0]), tiles * TILE), BF16),
    ]
    out_specs = [
        pl.BlockSpec((1, tok_count, TILE), lambda i: (behind(i), 0, 0)),
        pl.BlockSpec((held, TILE), lambda i: (0, behind(i))),
        pl.BlockSpec((out_shape[2].shape[0], TILE), lambda i: (0, behind(i))),
    ]
    shared_shape = [
        jax.ShapeDtypeStruct((tok_count, SPAN), BF16),
        jax.ShapeDtypeStruct((SPAN, tok_count), F32),
        jax.ShapeDtypeStruct((blocks, SPAN, 2 * SPAN), BF16),
    ]
    shared_specs = [whole(each.shape) for each in shared_shape]
    extras = 0 if extra is None else extra.shape[0]
    if extras:
        ins.append(extra)
        specs.append(pl.BlockSpec((extras, TILE), lambda i: (0, behind(i))))
    if leads:
        out_shape += shared_shape
        out_specs += shared_specs
    else:
        ins += shared
        specs += shared_specs
    outs = pl.pallas_call(
        lambda *refs: scan_kernel(leads, extras, tiles, len(pieces), lead_at, base, *refs),
        grid=(tiles + leads + 1,),
        in_specs=specs,
        out_specs=out_specs,
        out_shape=out_shape,
        scratch_shapes=[pltpu.VMEM((rows, depth), BF16)]
        + [pltpu.VMEM((depth, TILE), BF16)] * 2
        + [pltpu.VMEM((rows, TILE), F32)] * 2
        + [pltpu.SemaphoreType.DMA((4,))],
        compiler_params=params(),
        cost_estimate=pl.CostEstimate(flops=3_000_000_000 * tiles, bytes_accessed=3_000_000 * tiles, transcendentals=0),
        name="project_scan",
    )(*ins)
    return *outs[:3], (list(outs[3:]) if leads else shared)


def run_norm(out, place, y, c_rows, reach, gain, gather, state, first, base, tiles, width):
    tok_count = c_rows.shape[0]
    ins = [place, y, c_rows, reach, gain, gather, *state]
    specs = [
        pl.BlockSpec(memory_space=pltpu.SMEM),
        pl.BlockSpec((1, tok_count, TILE), lambda i: (i + base, 0, 0)),
        whole(c_rows.shape),
        pl.BlockSpec((1, tok_count, TILE), lambda i: (i + first, 0, 0)),
        pl.BlockSpec((1, TILE), lambda i: (0, i + first)),
        whole(gather.shape),
    ]
    specs += [pl.BlockSpec((part.shape[0], TILE), lambda i: (0, i + base)) for part in state]
    aliases = {}
    if out is not None:
        aliases = {len(ins): 0}
        ins.append(out)
        specs.append(pl.BlockSpec(memory_space=pl.ANY))
    return pl.pallas_call(
        lambda *refs: norm_kernel(len(state), *refs),
        grid=(tiles,),
        in_specs=specs,
        out_specs=pl.BlockSpec((tok_count, TILE), lambda i: (0, i + first)),
        out_shape=jax.ShapeDtypeStruct((tok_count, width), BF16),
        input_output_aliases=aliases,
        compiler_params=params(SMALL),
        cost_estimate=pl.CostEstimate(flops=400_000_000 * tiles, bytes_accessed=5 * tok_count * TILE * tiles, transcendentals=0),
        name="head_norm",
    )(*ins)


def shifted(value, z_by, y_by, z_count, y_count):
    pairs = []
    for z in range(z_count - z_by):
        for y in range(y_count):
            pairs.append((z * y_count + y, (z + z_by) * y_count + (y + y_by) % y_count))
    return lax.ppermute(value, "seq", pairs)


def stack(*arrays):
    return jnp.concatenate(arrays, axis=0)


def together(*arrays):
    return lax.optimization_barrier(arrays)


class Links:
    def __init__(self, z_count, y_count):
        self.z_count, self.y_count = z_count, y_count

    def index(self, x, core, z, y):
        return (x * 2 + core) * self.z_count * self.y_count + z * self.y_count + y

    def send(self, value, target):
        pairs = []
        for x in range(2):
            for core in range(2):
                for z in range(self.z_count):
                    for y in range(self.y_count):
                        pairs.append((self.index(x, core, z, y), self.index(*target(x, core, z, y))))
        return lax.ppermute(value, ("dp", "seq"), pairs)

    def along_z(self, value, by):
        return self.send(value, lambda x, core, z, y: (x, core, (z + by) % self.z_count, y))

    def first(self, value):
        return self.send(value, lambda x, core, z, y: (x, core, z, 1 - y) if core else (1 - x, core, z, y))

    def second(self, value):
        return self.send(value, lambda x, core, z, y: (1 - x, core, z, y) if core else (x, core, z, 1 - y))

    def sibling(self, value):
        return self.send(value, lambda x, core, z, y: (x, 1 - core, z, y))

    def gather(self, own, early, decays):
        z1, z3, own_1, own_2, own = together(
            self.along_z(own, 1), self.along_z(own, 3), self.first(own), self.second(own), own
        )
        near = stack(z1, z3)
        z2, near_1, near_2, own_12, *early = together(
            self.along_z(own, 2), self.first(near), self.second(near), self.second(own_1), *early
        )
        mine = stack(own, own_1, own_2, own_12)
        far_1, far_2, near_12, mine_other, *decays = together(
            self.first(z2), self.second(z2), self.second(near_1), self.sibling(mine), *decays(early)
        )
        beside = stack(near, near_1, near_2, near_12)
        far = stack(z2, far_1, far_2)
        far_12, beside_other, far_other = together(self.second(far_1), self.sibling(beside), self.sibling(far))
        return [mine, beside, far, far_12, mine_other, beside_other, far_other, self.sibling(far_12)], early, decays

    def owners(self):
        dp, seq = lax.axis_index("dp"), lax.axis_index("seq")
        x, core = dp // 2, dp % 2
        z, y = seq // self.y_count, seq % self.y_count
        places = []
        for at in (core, 1 - core):
            for hops in ((0,), (1, 3), (2,)):
                for by_first, by_second in ((0, 0), (1, 0), (0, 1), (1, 1)):
                    for hop in hops:
                        turn_x = jnp.where(at == 0, by_first, by_second)
                        turn_y = jnp.where(at == 0, by_second, by_first)
                        other = (z - hop + self.z_count) % self.z_count
                        places.append(self.index((x + turn_x) % 2, at, other, (y + turn_y) % 2))
        return jnp.stack(places).astype(jnp.int32)


def expand(per_head, head_size):
    return jnp.repeat(per_head, head_size, axis=-1)


def local(tokens, w_xbc, conv_weight, conv_bias, a_log, dt_in, d_skip, norm_gain):
    token_rows = tokens[0]
    tok_count = token_rows.shape[0]
    heads = a_log.shape[0]
    width_x = norm_gain.shape[0]
    head_size = width_x // heads
    channels = w_xbc.shape[1]
    blocks = tok_count // SPAN
    tiles = width_x // TILE
    per_tile = TILE // head_size
    seq_count = lax.axis_size("seq")
    z_count = 4
    y_count = seq_count // z_count
    y_mine = lax.rem(lax.axis_index("seq"), y_count)

    after = lambda rows: lax.ppermute(rows, "seq", [(i, i + 1) for i in range(seq_count - 1)])
    rim_rows = token_rows[tok_count - RIM :]
    taps = jnp.concatenate([conv_weight, conv_bias[None], jnp.zeros((3, channels), F32)], axis=0)
    rate = -LOG2E * jnp.exp(a_log)
    totals = rate[:, None] * jnp.sum(jax.nn.softplus(dt_in[0]).reshape(heads, blocks, SPAN), axis=2)
    head_of = jnp.arange(TILE) // head_size
    gather = jnp.where(head_of[:, None] == head_of[None, :], 1.0 / head_size, 0.0).astype(BF16)

    def lane_rows(totals):
        rows = jnp.concatenate([jnp.exp2(totals).T, d_skip[None]], axis=0)
        rows = jnp.pad(expand(rows, head_size), ((0, -(blocks + 1) % 8), (0, 0)))
        return rows.reshape(rows.shape[0], tiles, TILE).transpose(1, 0, 2)

    def along_y(totals):
        own = jnp.sum(totals, axis=1)
        side = jnp.broadcast_to(jnp.pad(own, (0, SPAN - heads))[None], (8, SPAN))
        return [own] + [shifted(side, 0, k, z_count, y_count)[0, :heads] for k in range(1, y_count)]

    def along_z(y_decay):
        own = jnp.broadcast_to(jnp.pad(sum(y_decay), (0, SPAN - heads))[None], (8, SPAN))
        return [shifted(own, k, 0, z_count, y_count)[0, :heads] for k in range(1, z_count - 1)]

    def z_weights(z_decay):
        reach = [jnp.zeros((heads,), F32)]
        for decay in z_decay:
            reach.append(reach[-1] + decay)
        return reach[1:]

    by_block = lambda rows: rows.reshape(tiles, per_tile, blocks, -1).swapaxes(1, 2).reshape(tiles, blocks * per_tile, -1)
    raw = by_block(dt_in[0])
    rates = by_block(jnp.broadcast_to(rate[:, None], (heads, blocks)))
    lanes = lane_rows(totals)
    if lax.axis_size("dp") == 4 and seq_count == 8:
        split = tiles // 2
        links = Links(z_count, y_count)
        row_count = w_xbc.shape[0]
        by_column = w_xbc.reshape(row_count, channels // TILE, TILE).swapaxes(0, 1)[None]
        late_w = lax.all_gather(by_column[:, :split], ("dp", "seq"), axis=0, tiled=True)
        late_rows = jnp.arange(lax.axis_size("dp") * seq_count, dtype=jnp.int32) * row_count
        early_rows = links.owners() * row_count

        kept = expand(jnp.exp2(jnp.sum(totals, axis=1)), head_size)
        wide = (tiles - split) * TILE
        rest = jnp.pad(kept[: split * TILE], (0, -(split * TILE) % wide)).reshape(-1, wide)
        own_kept = jnp.concatenate([kept[None, split * TILE :], rest], axis=0)
        extra = jnp.pad(own_kept, ((0, 16 - own_kept.shape[0]), (0, 0))).astype(BF16)

        early_w, prepared, (decay, grow, reach, tails) = links.gather(
            by_column[:, split:],
            (taps, lanes, gather, early_rows, late_rows, after(rim_rows), own_kept, extra, raw, rates),
            lambda ready: run_decay(*ready[8:]),
        )
        taps, lanes, gather, early_rows, late_rows, rim, own_kept, extra = prepared[:8]
        calls = [(early_w, early_rows, split, 0, tiles - split), ([late_w], late_rows, 0, 0, split)]
        lead_at = tiles - split
        halved = y_mine.astype(jnp.int32)[None]

        upper = y_mine == 1
        swap = lambda value: shifted(value, 0, 1, z_count, y_count)

        half = SPAN // 2

        def plane_of(own, other, upper_kept, rows=None):
            other = other[:half].astype(F32)
            plane = jnp.where(upper, own + upper_kept * other, upper_kept * own + other)
            if rows is not None:
                plane = jnp.concatenate([plane, jnp.pad(rows, ((0, 16 - rows.shape[0]), (0, 0)))], axis=0)
            plane = plane.astype(BF16)
            return [shifted(plane, k, 0, z_count, y_count) for k in range(1, z_count)]

        def halves_of(own, other, below, lower_kept, z_kept):
            base = below[0][:half].astype(F32)
            through = 1.0
            for kept, part in zip(z_kept, below[1:]):
                through = through * kept
                base = base + through * part[:half].astype(F32)
            above = lower_kept * base + jnp.where(upper, other[:half].astype(F32), own)
            theirs = swap(jnp.where(upper, base, above).astype(BF16))
            return [jnp.where(upper, above, base).astype(BF16), theirs]

    else:
        full = lax.all_gather(w_xbc, ("dp", "seq"), axis=0, tiled=True)
        full = full.reshape(full.shape[0], channels // TILE, TILE).swapaxes(0, 1)[None]
        first_row = jnp.zeros((1,), jnp.int32)
        calls = [([full], first_row, first, first, min(5, tiles - first)) for first in range(0, tiles, 5)]
        lead_at = tiles
        rim = after(rim_rows)
        halved = None
        decay, grow, reach, tails = run_decay(raw, rates)
        y_decay = along_y(totals)
        z_reach = z_weights(along_z(y_decay))

        def beside(sent):
            return [shifted(sent, 0, k, z_count, y_count) for k in range(1, y_count)]

        def incoming(own, parts, lane):
            place = [lax.rem(y_mine - k + y_count, y_count) for k in range(y_count)]
            spread_lanes = lambda row: expand(row, head_size)[lane]
            inner = lambda keep: sum(jnp.where(keep(m), y_decay[m], 0.0) for m in range(y_count))
            parts = [own] + [part.astype(F32) for part in parts]
            plane, above = 0.0, 0.0
            for k, part in enumerate(parts):
                after = inner(lambda m: place[m] > place[k])
                until = inner(lambda m: (place[m] > place[k]) & (place[m] < y_mine))
                plane = plane + spread_lanes(jnp.exp2(after)) * part
                above = above + spread_lanes(jnp.where(place[k] < y_mine, jnp.exp2(until), 0.0)) * part
            inside = inner(lambda m: place[m] < y_mine)
            plane = plane.astype(BF16)
            for k in range(1, z_count):
                along = inside if k == 1 else inside + z_reach[k - 2]
                above = above + spread_lanes(jnp.exp2(along)) * shifted(plane, k, 0, z_count, y_count).astype(F32)
            return [above.astype(BF16)]

    def scan(call, shared, extra=None):
        pieces, places, first, base, count = call
        return run_scan(
            pieces, places, halved, lead_at, base, rim, token_rows, taps, shared, decay, grow, tails, lanes, first, count, extra
        )

    def norm(out, y, state, first, base, count):
        place = y_mine.astype(jnp.int32)[None]
        return run_norm(
            out, place, y, shared[0], reach, norm_gain[None], gather, state, first + base, base, count, width_x
        )

    if halved is None:
        shared, out = None, None
        pending = []
        for call in calls:
            y, own, sent, shared = scan(call, shared)
            first, count = call[2], call[4]
            pending.append((y, incoming(own, beside(sent), slice(first * TILE, (first + count) * TILE)), first, 0, count))
        for each in pending:
            out = norm(out, *each)
        return out[None]

    (_, _, first_a, _, count_a), (_, _, first_b, _, count_b) = calls
    y_a, own_a, sent_a, shared = scan(calls[0], None, extra)
    other_a = swap(sent_a)
    kept_rows = slice(half, half + own_kept.shape[0])
    later = lambda rows: rows[1:].reshape(-1)[: count_b * TILE]
    other_kept = other_a[kept_rows].astype(F32)
    lower_kept = jnp.where(upper, other_kept, own_kept)
    upper_kept = jnp.where(upper, own_kept, other_kept)
    pieces, other_a = together(calls[1][0], other_a)
    below_a = plane_of(own_a, other_a, upper_kept[0], lower_kept * upper_kept)
    y_b, own_b, sent_b, _ = scan((pieces, *calls[1][1:]), shared)
    sent_b, *below_a = together(sent_b, *below_a)
    other_b = swap(sent_b)
    z_kept = [part[kept_rows].astype(F32) for part in below_a]
    state_a = halves_of(own_a, other_a, below_a, lower_kept[0], [kept[0] for kept in z_kept])
    below_b = plane_of(own_b, other_b, later(upper_kept))
    out = norm(None, y_a, state_a, first_a, 0, count_a // 2)
    out = norm(out, y_a, state_a, first_a, count_a // 2, count_a - count_a // 2)
    out, *below_b = together(out, *below_b)
    state_b = halves_of(own_b, other_b, below_b, later(lower_kept), [later(kept) for kept in z_kept])
    out = norm(out, y_b, state_b, first_b, 0, count_b)
    return out[None]


def solution(mesh):
    return jax.shard_map(
        local,
        mesh=mesh,
        in_specs=(
            P("dp", "seq", None),
            P(("dp", "seq"), None),
            P(),
            P(),
            P(),
            P("dp", None, "seq"),
            P(),
            P(),
        ),
        out_specs=P("dp", "seq", None),
        check_vma=False,
    )
```
